128 devices in a mesh: depth: 4 (over y), tile: 32 (over z, x, core).
Axes of the slice: x: 4, y: 4, z: 4, core: 2. Of those that a mesh axis runs over, the one named last changes fastest.
Arguments:
- field: float32 [128, 2048, 2048], P('depth', 'tile'), may hold values from -1 to 1
- absorb_coef: float32 [2], replicated, may hold values from 0.01 to 0.04
- color_coef: float32 [3, 4], replicated, may hold values from -1 to 1
- light: float32 [3], replicated, may hold values from -1 to 1
Outputs:
- image: float32 [4, 2048, 2048], P(None, 'tile', 'depth')
The draws below stay inside these ranges and needn't reach their ends.
All inputs are finite; a program needn't handle non-finite values.
Results may differ from the reference program's by a relative error of at most 0.0003.
Values sent between devices are 32-bit elements; how exact they have to be, the bound alone decides.
A program may use at most 192 MiB of HBM per device.

```python
import math
import jax
import jax.numpy as jnp
from jax import lax

NY = 2048
NX = 2048
NZ = 128


def level_of(key, extent, pieces, least, largest):
    def one(position, parts):
        steps = jax.random.uniform(jax.random.fold_in(jax.random.fold_in(key, 6), position), (parts,), jnp.float32, least / len(pieces), largest / len(pieces))
        return jnp.repeat(jnp.exp(steps), extent[position] // parts).reshape((-1,) + (1,) * (len(extent) - position - 1))

    gain = one(*pieces[0])
    for cut in pieces[1:]:
        gain = gain * one(*cut)
    return gain


def setup_inputs(seed: int = 0) -> dict:
    key_list = jax.random.split(jax.random.key(seed), 5)
    return {
        "field": jnp.clip(jax.random.uniform(key_list[0], (NZ, NX, NY), jnp.float32, -1.0, 1.0) * level_of(key_list[0], (NZ, NX, NY), ((0, 4), (1, 32)), -0.4, 0.0), -1.0, 1.0),
        "absorb_coef": jnp.clip(jnp.exp(jax.random.uniform(key_list[1], (2,), jnp.float32, math.log(0.01), math.log(0.04))), 0.01, 0.04),
        "color_coef": jnp.clip(jax.random.uniform(key_list[2], (3, 4), jnp.float32, -1.0, 1.0), -1.0, 1.0),
        "light": jnp.clip(jax.random.uniform(key_list[3], (3,), jnp.float32, -1.0, 1.0), -1.0, 1.0),
    }


def slice_light(below, padded_here, above, absorb_coef, color_coef, light):
    center = padded_here[1:-1]
    grad_z = 0.5 * (above - below)
    grad_x = 0.5 * (padded_here[2:] - padded_here[:-2])
    side_pad = jnp.pad(center, ((0, 0), (1, 1)))
    grad_y = 0.5 * (side_pad[:, 2:] - side_pad[:, :-2])
    facing = jnp.abs(light[0] * grad_z + light[1] * grad_x + light[2] * grad_y)
    shade = facing / jnp.sqrt(grad_z * grad_z + grad_x * grad_x + grad_y * grad_y + 1.0)
    sigma = absorb_coef[0] + absorb_coef[1] * center * center
    coef = color_coef[:, :, None, None]
    poly = coef[:, 0] + center * (coef[:, 1] + center * (coef[:, 2] + center * coef[:, 3]))
    return (sigma, shade[None] * poly)

def reference(field, absorb_coef, color_coef, light):
    depth_total = field.shape[0]

    def march(carry, index):
        color, optical = carry
        here = lax.dynamic_index_in_dim(field, index, 0, keepdims=False)
        below = lax.dynamic_index_in_dim(field, jnp.maximum(index - 1, 0), 0, keepdims=False)
        below = below * (index > 0).astype(jnp.float32)
        above = lax.dynamic_index_in_dim(field, jnp.minimum(index + 1, depth_total - 1), 0, keepdims=False)
        above = above * (index < depth_total - 1).astype(jnp.float32)
        padded_here = jnp.pad(here, ((1, 1), (0, 0)))
        sigma, emitted = slice_light(below, padded_here, above, absorb_coef, color_coef, light)
        weight = (1.0 - jnp.exp(-sigma)) * jnp.exp(-optical)
        return ((color + emitted * weight[None], optical + sigma), None)
    start = (jnp.zeros((3,) + field.shape[1:], jnp.float32), jnp.zeros(field.shape[1:], jnp.float32))
    (color, optical), unused = lax.scan(march, start, jnp.arange(depth_total, dtype=jnp.int32))
    return jnp.concatenate([color, (1.0 - jnp.exp(-optical))[None]], axis=0)
```

```python
import functools
import math

import jax
import jax.numpy as jnp
from jax import lax
from jax.experimental import pallas as pl
from jax.experimental.pallas import tpu as pltpu
from jax.sharding import PartitionSpec as P

MESH = pl.DeviceIdType.MESH
LANES = 128
SUB = 8
TOP = 8
GROUP = 4
UNROLL = 2


def march(f_ref, j, dst, absorb_ref, color_ref, light_ref, slices, rows):
    lane = lax.broadcasted_iota(jnp.int32, (SUB, LANES), 1)
    first, last = lane == 0, lane == LANES - 1
    base = -absorb_ref[0] * math.log2(math.e)
    slope = -absorb_ref[1] * math.log2(math.e)
    lz, lx, ly = light_ref[0], light_ref[1], light_ref[2]
    for top in range(0, rows, GROUP * SUB):
        starts = [TOP + top + SUB * r for r in range(GROUP)]

        def step(i, carry):
            state = [list(carry[5 * r : 5 * r + 5]) for r in range(GROUP)]
            z0 = 1 + i * UNROLL
            for r, row in enumerate(starts):
                here = [f_ref[j + 1, z0 + u - 1, pl.ds(row, SUB), :] for u in range(UNROLL + 2)]
                for u in range(UNROLL):
                    z = z0 + u
                    below, f, above = here[u], here[u + 1], here[u + 2]
                    dz = above - below
                    dx = f_ref[j + 1, z, pl.ds(row + 1, SUB), :] - f_ref[j + 1, z, pl.ds(row - 1, SUB), :]
                    left = jnp.where(last, f_ref[j, z, pl.ds(row, SUB), :], f)
                    right = jnp.where(first, f_ref[j + 2, z, pl.ds(row, SUB), :], f)
                    dy = pltpu.roll(right, LANES - 1, 1) - pltpu.roll(left, 1, 1)
                    facing = jnp.abs(lz * dz + lx * dx + ly * dy)
                    shade = facing * lax.rsqrt((dz * dz + 4.0) + (dx * dx + dy * dy))
                    f2 = f * f
                    t, m0, m1, m2, m3 = state[r]
                    behind = t * jnp.exp2(base + slope * f2)
                    w0 = (t - behind) * shade
                    w1 = w0 * f
                    state[r] = [behind, m0 + w0, m1 + w1, m2 + w0 * f2, m3 + w1 * f2]
            return tuple(v for s in state for v in s)

        one = jnp.ones((SUB, LANES), jnp.float32)
        zero = jnp.zeros((SUB, LANES), jnp.float32)
        carry = lax.fori_loop(0, slices // UNROLL, step, (one, zero, zero, zero, zero) * GROUP)
        for r in range(GROUP):
            t, m0, m1, m2, m3 = carry[5 * r : 5 * r + 5]
            at = pl.ds(top + SUB * r, SUB)
            for c in range(3):
                dst[c, at, :] = (color_ref[c, 0] * m0 + color_ref[c, 1] * m1) + (
                    color_ref[c, 2] * m2 + color_ref[c, 3] * m3
                )
            dst[3, at, :] = t


def kernel(
    depths, tiles, slices, rows, blocks,
    field, absorb, color, light, out,
    f_ref, mine, image,
    load_sem, z_send, z_recv, x_send, x_recv, i_send, i_recv,
):
    d, t = lax.axis_index("depth"), lax.axis_index("tile")
    per = blocks // depths
    has_below, has_above = d > 0, d < depths - 1
    has_prev, has_next = t > 0, t < tiles - 1

    def load(j):
        return pltpu.make_async_copy(
            field.at[:, :, pl.ds(pl.multiple_of(j * LANES, LANES), LANES)],
            f_ref.at[j + 1, pl.ds(1, slices), pl.ds(TOP, rows), :],
            load_sem.at[j],
        )

    for j in range(blocks):
        load(j).start()

    barrier = pltpu.get_barrier_semaphore()
    for off in range(1, depths):
        pl.semaphore_signal(barrier, inc=1, device_id=(lax.rem(d + off, depths), t), device_id_type=MESH)
    for off in (1, tiles - 1):
        pl.semaphore_signal(barrier, inc=1, device_id=(d, lax.rem(t + off, tiles)), device_id_type=MESH)

    zeros = jnp.zeros((SUB, LANES), jnp.float32)
    for edge in (0, blocks + 1):

        def clear(z, _):
            for row in range(0, rows, SUB):
                f_ref[edge, z + 1, pl.ds(TOP + row, SUB), :] = zeros
            return 0

        lax.fori_loop(0, slices, clear, 0)
    for present, z in ((has_below, 0), (has_above, slices + 1)):

        @pl.when(jnp.logical_not(present))
        def _():
            def clear(j, _):
                for row in range(0, rows, SUB):
                    f_ref[j + 1, z, pl.ds(TOP + row, SUB), :] = zeros
                return 0

            lax.fori_loop(0, blocks, clear, 0)

    for present, row in ((has_prev, TOP - SUB), (has_next, TOP + rows)):

        @pl.when(jnp.logical_not(present))
        def _():
            def clear(j, _):
                for z in range(slices):
                    f_ref[j + 1, z + 1, pl.ds(row, SUB), :] = zeros
                return 0

            lax.fori_loop(0, blocks, clear, 0)

    pl.semaphore_wait(barrier, depths + 1)

    def order(owner_of, s):
        pick = lax.rem(s, depths - 1)
        off = jnp.where(pick == 0, 2, jnp.where(pick == 1, 1, 3))
        owner = lax.rem(owner_of + off, depths)
        own = s >= (depths - 1) * per
        k = jnp.where(own, s - (depths - 1) * per, s // (depths - 1))
        owner = jnp.where(own, owner_of, owner)
        return owner, k, owner * per + k

    def z_copy(way, j):
        src, dst = ((slices - 1, 0), (0, slices + 1))[way]
        return pltpu.make_async_remote_copy(
            src_ref=field.at[src, :, pl.ds(pl.multiple_of(j * LANES, LANES), LANES)],
            dst_ref=f_ref.at[j + 1, dst, pl.ds(TOP, rows), :],
            send_sem=z_send.at[way, j],
            recv_sem=z_recv.at[way, j],
            device_id=(lax.rem(d + (1, depths - 1)[way], depths), t),
            device_id_type=MESH,
        )

    def x_copy(way, j):
        src, dst = ((rows - 1, TOP - 1), (0, TOP + rows))[way]
        return pltpu.make_async_remote_copy(
            src_ref=field.at[:, pl.ds(src, 1), pl.ds(pl.multiple_of(j * LANES, LANES), LANES)],
            dst_ref=f_ref.at[j + 1, pl.ds(1, slices), pl.ds(dst, 1), :],
            send_sem=x_send.at[way, j],
            recv_sem=x_recv.at[way, j],
            device_id=(d, lax.rem(t + (1, tiles - 1)[way], tiles)),
            device_id_type=MESH,
        )

    sends = ((z_copy, 0, has_above, d + 1), (z_copy, 1, has_below, d - 1 + depths),
             (x_copy, 0, has_next, d), (x_copy, 1, has_prev, d))
    recvs = ((z_copy, 0, has_below), (z_copy, 1, has_above), (x_copy, 0, has_prev), (x_copy, 1, has_next))

    def start(s, _):
        for copy, way, present, to in sends:

            @pl.when(present)
            def _():
                copy(way, order(lax.rem(to, depths), s)[2]).start()

        return 0

    lax.fori_loop(0, blocks, start, 0)
    for j in range(blocks):
        load(j).wait()

    def image_copy(s, owner, k):
        return pltpu.make_async_remote_copy(
            src_ref=mine.at[s],
            dst_ref=image.at[d, k],
            send_sem=i_send.at[s],
            recv_sem=i_recv.at[d, k],
            device_id=(owner, t),
            device_id_type=MESH,
        )

    def arrive(j):
        for copy, way, present in recvs:

            @pl.when(present)
            def _():
                copy(way, j).wait_recv()

    def remote(s, _):
        owner, k, j = order(d, s)
        arrive(j)
        march(f_ref, j, mine.at[s], absorb, color, light, slices, rows)
        image_copy(s, owner, k).start()
        return 0

    lax.fori_loop(0, (depths - 1) * per, remote, 0)

    def local(k, _):
        j = d * per + k
        arrive(j)
        march(f_ref, j, image.at[d, k], absorb, color, light, slices, rows)
        return 0

    lax.fori_loop(0, per, local, 0)

    for k in range(per):
        for off in range(1, depths):
            q = lax.rem(d + off, depths)
            pltpu.make_async_remote_copy(
                src_ref=mine.at[0],
                dst_ref=image.at[q, k],
                send_sem=i_send.at[0],
                recv_sem=i_recv.at[q, k],
                device_id=(q, t),
                device_id_type=MESH,
            ).wait_recv()

        def compose(i, _):
            at = pl.ds(pl.multiple_of(i * SUB, SUB), SUB)
            seen = image[0, k, 3, at, :]
            total = [image[0, k, c, at, :] for c in range(3)]
            for q in range(1, depths):
                total = [total[c] + seen * image[q, k, c, at, :] for c in range(3)]
                seen = seen * image[q, k, 3, at, :]
            for c in range(3):
                out[c, at, k * LANES : (k + 1) * LANES] = total[c]
            out[3, at, k * LANES : (k + 1) * LANES] = 1.0 - seen
            return 0

        lax.fori_loop(0, rows // SUB, compose, 0)

    def drain(s, _):
        for copy, way, present, _to in sends:

            @pl.when(present)
            def _():
                copy(way, s).wait_send()

        return 0

    lax.fori_loop(0, blocks, drain, 0)

    def drain_images(s, _):
        image_copy(s, lax.rem(d + 1, depths), 0).wait_send()
        return 0

    lax.fori_loop(0, (depths - 1) * per, drain_images, 0)


def on_device(depths, tiles, field, absorb, color, light):
    slices, rows, columns = field.shape
    blocks = columns // LANES
    per = blocks // depths
    smem = pl.BlockSpec(memory_space=pltpu.SMEM)
    return pl.pallas_call(
        functools.partial(kernel, depths, tiles, slices, rows, blocks),
        out_shape=jax.ShapeDtypeStruct((4, rows, columns // depths), jnp.float32),
        in_specs=[pl.BlockSpec(memory_space=pl.ANY), smem, smem, smem],
        out_specs=pl.BlockSpec(memory_space=pltpu.VMEM),
        scratch_shapes=[
            pltpu.VMEM((blocks + 2, slices + 2, rows + 2 * TOP, LANES), jnp.float32),
            pltpu.VMEM(((depths - 1) * per, 4, rows, LANES), jnp.float32),
            pltpu.VMEM((depths, per, 4, rows, LANES), jnp.float32),
            pltpu.SemaphoreType.DMA((blocks,)),
            pltpu.SemaphoreType.DMA((2, blocks)),
            pltpu.SemaphoreType.DMA((2, blocks)),
            pltpu.SemaphoreType.DMA((2, blocks)),
            pltpu.SemaphoreType.DMA((2, blocks)),
            pltpu.SemaphoreType.DMA(((depths - 1) * per,)),
            pltpu.SemaphoreType.DMA((depths, per)),
        ],
        compiler_params=pltpu.CompilerParams(
            collective_id=0, has_side_effects=True, vmem_limit_bytes=48 << 20
        ),
    )(field, absorb, color, light)


def solution(mesh):
    depths, tiles = mesh.shape["depth"], mesh.shape["tile"]
    return jax.shard_map(
        functools.partial(on_device, depths, tiles),
        mesh=mesh,
        in_specs=(P("depth", "tile", None), P(), P(), P()),
        out_specs=P(None, "tile", "depth"),
        check_vma=False,
    )
```

```python
import functools
import math

import jax
import jax.numpy as jnp
from jax import lax
from jax.experimental import pallas as pl
from jax.experimental.pallas import tpu as pltpu
from jax.sharding import PartitionSpec as P

MESH = pl.DeviceIdType.MESH
LANES = 128
SUB = 8
TOP = 8
GROUP = 2
UNROLL = 16


def march(f_ref, j, dst, absorb_ref, color_ref, light_ref, slices, rows):
    lane = lax.broadcasted_iota(jnp.int32, (SUB, LANES), 1)
    first, last = lane == 0, lane == LANES - 1
    base = -absorb_ref[0] * math.log2(math.e)
    slope = -absorb_ref[1] * math.log2(math.e)
    lz, lx, ly = light_ref[0], light_ref[1], light_ref[2]
    for top in range(0, rows, GROUP * SUB):
        starts = [TOP + top + SUB * r for r in range(GROUP)]

        def sideways(z0):
            found = []
            for row in starts:
                for u in range(UNROLL):
                    f = f_ref[j + 1, z0 + u, pl.ds(row, SUB), :]
                    left = jnp.where(last, f_ref[j, z0 + u, pl.ds(row, SUB), :], f)
                    right = jnp.where(first, f_ref[j + 2, z0 + u, pl.ds(row, SUB), :], f)
                    found.append(pltpu.roll(right, LANES - 1, 1) - pltpu.roll(left, 1, 1))
            return found

        def chunk(z0, state, across):
            state = [list(state[5 * r : 5 * r + 5]) for r in range(GROUP)]
            for r, row in enumerate(starts):
                here = [f_ref[j + 1, z0 + u - 1, pl.ds(row, SUB), :] for u in range(UNROLL + 2)]
                for u in range(UNROLL):
                    below, f, above = here[u], here[u + 1], here[u + 2]
                    dz = above - below
                    dx = f_ref[j + 1, z0 + u, pl.ds(row + 1, SUB), :] - f_ref[j + 1, z0 + u, pl.ds(row - 1, SUB), :]
                    dy = across[r * UNROLL + u]
                    facing = jnp.abs(lz * dz + lx * dx + ly * dy)
                    shade = facing * lax.rsqrt((dz * dz + 4.0) + (dx * dx + dy * dy))
                    f2 = f * f
                    t, m0, m1, m2, m3 = state[r]
                    behind = t * jnp.exp2(base + slope * f2)
                    w0 = (t - behind) * shade
                    w1 = w0 * f
                    state[r] = [behind, m0 + w0, m1 + w1, m2 + w0 * f2, m3 + w1 * f2]
            return [v for s in state for v in s]

        def step(i, carry):
            z0 = 1 + i * UNROLL
            ahead = sideways(z0 + UNROLL)
            return tuple(chunk(z0, carry[: 5 * GROUP], carry[5 * GROUP :]) + ahead)

        one = jnp.ones((SUB, LANES), jnp.float32)
        zero = jnp.zeros((SUB, LANES), jnp.float32)
        carry = lax.fori_loop(
            0, slices // UNROLL - 1, step, (one, zero, zero, zero, zero) * GROUP + tuple(sideways(1))
        )
        carry = chunk(1 + slices - UNROLL, carry[: 5 * GROUP], carry[5 * GROUP :])
        for r in range(GROUP):
            t, m0, m1, m2, m3 = carry[5 * r : 5 * r + 5]
            at = pl.ds(top + SUB * r, SUB)
            for c in range(3):
                dst[c, at, :] = (color_ref[c, 0] * m0 + color_ref[c, 1] * m1) + (
                    color_ref[c, 2] * m2 + color_ref[c, 3] * m3
                )
            dst[3, at, :] = t


def kernel(
    depths, tiles, slices, rows, blocks,
    field, absorb_in, color_in, light_in, out,
    f_ref, mine, image, absorb, color, light, param_sem,
    load_sem, z_send, z_recv, x_send, x_recv, i_send, i_recv,
):
    d, t = lax.axis_index("depth"), lax.axis_index("tile")
    per = blocks // depths
    has_below, has_above = d > 0, d < depths - 1
    has_prev, has_next = t > 0, t < tiles - 1

    def load(j):
        return pltpu.make_async_copy(
            field.at[:, :, pl.ds(pl.multiple_of(j * LANES, LANES), LANES)],
            f_ref.at[j + 1, pl.ds(1, slices), pl.ds(TOP, rows), :],
            load_sem.at[j],
        )

    params = [
        pltpu.make_async_copy(src, dst, param_sem.at[i])
        for i, (src, dst) in enumerate(((absorb_in, absorb), (color_in, color), (light_in, light)))
    ]
    for copy in params:
        copy.start()
    for j in range(blocks):
        load(j).start()

    barrier = pltpu.get_barrier_semaphore()
    for off in range(1, depths):
        pl.semaphore_signal(barrier, inc=1, device_id=(lax.rem(d + off, depths), t), device_id_type=MESH)
    for off in (1, tiles - 1):
        pl.semaphore_signal(barrier, inc=1, device_id=(d, lax.rem(t + off, tiles)), device_id_type=MESH)

    zeros = jnp.zeros((SUB, LANES), jnp.float32)
    for edge in (0, blocks + 1):

        def clear(z, _):
            for row in range(0, rows, SUB):
                f_ref[edge, z + 1, pl.ds(TOP + row, SUB), :] = zeros
            return 0

        lax.fori_loop(0, slices, clear, 0)
    for present, z in ((has_below, 0), (has_above, slices + 1)):

        @pl.when(jnp.logical_not(present))
        def _():
            def clear(j, _):
                for row in range(0, rows, SUB):
                    f_ref[j + 1, z, pl.ds(TOP + row, SUB), :] = zeros
                return 0

            lax.fori_loop(0, blocks, clear, 0)

    for present, row in ((has_prev, TOP - SUB), (has_next, TOP + rows)):

        @pl.when(jnp.logical_not(present))
        def _():
            def clear(j, _):
                for z in range(slices):
                    f_ref[j + 1, z + 1, pl.ds(row, SUB), :] = zeros
                return 0

            lax.fori_loop(0, blocks, clear, 0)

    pl.semaphore_wait(barrier, depths + 1)

    def order(owner_of, s):
        pick = lax.rem(s, depths - 1)
        off = jnp.where(pick == 0, 2, jnp.where(pick == 1, 1, 3))
        owner = lax.rem(owner_of + off, depths)
        own = s >= (depths - 1) * per
        k = jnp.where(own, s - (depths - 1) * per, s // (depths - 1))
        owner = jnp.where(own, owner_of, owner)
        return owner, k, owner * per + k

    def z_copy(way, j):
        src, dst = ((slices - 1, 0), (0, slices + 1))[way]
        return pltpu.make_async_remote_copy(
            src_ref=field.at[src, :, pl.ds(pl.multiple_of(j * LANES, LANES), LANES)],
            dst_ref=f_ref.at[j + 1, dst, pl.ds(TOP, rows), :],
            send_sem=z_send.at[way, j],
            recv_sem=z_recv.at[way, j],
            device_id=(lax.rem(d + (1, depths - 1)[way], depths), t),
            device_id_type=MESH,
        )

    def x_copy(way, j):
        src, dst = ((rows - 1, TOP - 1), (0, TOP + rows))[way]
        return pltpu.make_async_remote_copy(
            src_ref=field.at[:, pl.ds(src, 1), pl.ds(pl.multiple_of(j * LANES, LANES), LANES)],
            dst_ref=f_ref.at[j + 1, pl.ds(1, slices), pl.ds(dst, 1), :],
            send_sem=x_send.at[way, j],
            recv_sem=x_recv.at[way, j],
            device_id=(d, lax.rem(t + (1, tiles - 1)[way], tiles)),
            device_id_type=MESH,
        )

    sends = ((z_copy, 0, has_above, d + 1), (z_copy, 1, has_below, d - 1 + depths),
             (x_copy, 0, has_next, d), (x_copy, 1, has_prev, d))
    recvs = ((z_copy, 0, has_below), (z_copy, 1, has_above), (x_copy, 0, has_prev), (x_copy, 1, has_next))

    def start(s, _):
        for copy, way, present, to in sends:

            @pl.when(present)
            def _():
                copy(way, order(lax.rem(to, depths), s)[2]).start()

        return 0

    lax.fori_loop(0, blocks, start, 0)
    for copy in params:
        copy.wait()
    for j in range(blocks):
        load(j).wait()

    def image_copy(s, owner, k):
        return pltpu.make_async_remote_copy(
            src_ref=mine.at[s],
            dst_ref=image.at[d, k],
            send_sem=i_send.at[s],
            recv_sem=i_recv.at[d, k],
            device_id=(owner, t),
            device_id_type=MESH,
        )

    def arrive(j):
        for copy, way, present in recvs:

            @pl.when(present)
            def _():
                copy(way, j).wait_recv()

    def remote(s, _):
        owner, k, j = order(d, s)
        arrive(j)
        march(f_ref, j, mine.at[s], absorb, color, light, slices, rows)
        image_copy(s, owner, k).start()
        return 0

    lax.fori_loop(0, (depths - 1) * per, remote, 0)

    def local(k, _):
        j = d * per + k
        arrive(j)
        march(f_ref, j, image.at[d, k], absorb, color, light, slices, rows)
        return 0

    lax.fori_loop(0, per, local, 0)

    for k in range(per):
        for off in range(1, depths):
            q = lax.rem(d + off, depths)
            pltpu.make_async_remote_copy(
                src_ref=mine.at[0],
                dst_ref=image.at[q, k],
                send_sem=i_send.at[0],
                recv_sem=i_recv.at[q, k],
                device_id=(q, t),
                device_id_type=MESH,
            ).wait_recv()

        def compose(i, _):
            at = pl.ds(pl.multiple_of(i * SUB, SUB), SUB)
            seen = image[0, k, 3, at, :]
            total = [image[0, k, c, at, :] for c in range(3)]
            for q in range(1, depths):
                total = [total[c] + seen * image[q, k, c, at, :] for c in range(3)]
                seen = seen * image[q, k, 3, at, :]
            for c in range(3):
                out[c, at, k * LANES : (k + 1) * LANES] = total[c]
            out[3, at, k * LANES : (k + 1) * LANES] = 1.0 - seen
            return 0

        lax.fori_loop(0, rows // SUB, compose, 0)

    def drain(s, _):
        for copy, way, present, _to in sends:

            @pl.when(present)
            def _():
                copy(way, s).wait_send()

        return 0

    lax.fori_loop(0, blocks, drain, 0)

    def drain_images(s, _):
        image_copy(s, lax.rem(d + 1, depths), 0).wait_send()
        return 0

    lax.fori_loop(0, (depths - 1) * per, drain_images, 0)


def on_device(depths, tiles, field, absorb, color, light):
    slices, rows, columns = field.shape
    blocks = columns // LANES
    per = blocks // depths
    return pl.pallas_call(
        functools.partial(kernel, depths, tiles, slices, rows, blocks),
        out_shape=jax.ShapeDtypeStruct((4, rows, columns // depths), jnp.float32),
        in_specs=[pl.BlockSpec(memory_space=pl.ANY)] * 4,
        out_specs=pl.BlockSpec(memory_space=pltpu.VMEM),
        scratch_shapes=[
            pltpu.VMEM((blocks + 2, slices + 2, rows + 2 * TOP, LANES), jnp.float32),
            pltpu.VMEM(((depths - 1) * per, 4, rows, LANES), jnp.float32),
            pltpu.VMEM((depths, per, 4, rows, LANES), jnp.float32),
            pltpu.SMEM((2,), jnp.float32),
            pltpu.SMEM((3, 4), jnp.float32),
            pltpu.SMEM((3,), jnp.float32),
            pltpu.SemaphoreType.DMA((3,)),
            pltpu.SemaphoreType.DMA((blocks,)),
            pltpu.SemaphoreType.DMA((2, blocks)),
            pltpu.SemaphoreType.DMA((2, blocks)),
            pltpu.SemaphoreType.DMA((2, blocks)),
            pltpu.SemaphoreType.DMA((2, blocks)),
            pltpu.SemaphoreType.DMA(((depths - 1) * per,)),
            pltpu.SemaphoreType.DMA((depths, per)),
        ],
        compiler_params=pltpu.CompilerParams(
            collective_id=0, has_side_effects=True, vmem_limit_bytes=60 << 20
        ),
    )(field, absorb, color, light)


def solution(mesh):
    depths, tiles = mesh.shape["depth"], mesh.shape["tile"]
    return jax.shard_map(
        functools.partial(on_device, depths, tiles),
        mesh=mesh,
        in_specs=(P("depth", "tile", None), P(), P(), P()),
        out_specs=P(None, "tile", "depth"),
        check_vma=False,
    )
```

```python
import functools
import math

import jax
import jax.numpy as jnp
from jax import lax
from jax.experimental import pallas as pl
from jax.experimental.pallas import tpu as pltpu
from jax.sharding import PartitionSpec as P

MESH = pl.DeviceIdType.MESH
LANES = 128
SUB = 8
TOP = 8
Z0 = 2
GROUP = 2
UNROLL = 16
LAG = 4
SPLIT = 3


class Shading:
    def __init__(self, absorb, color, light):
        self.base = -absorb[0] * math.log2(math.e)
        self.slope = -absorb[1] * math.log2(math.e)
        self.light = light[0], light[1], light[2]
        self.color = color

    def facing_and_norm(self, dz, dx, dy):
        lz, lx, ly = self.light
        facing = jnp.abs(lz * dz + lx * dx + ly * dy)
        return facing * lax.rsqrt((dz * dz + 4.0) + (dx * dx + dy * dy))

    def channel(self, c, m0, m1, m2, m3):
        color = self.color
        return (color[c, 0] * m0 + color[c, 1] * m1) + (color[c, 2] * m2 + color[c, 3] * m3)


def sideways(f_ref, j, z, row):
    lane = lax.broadcasted_iota(jnp.int32, (SUB, LANES), 1)
    f = f_ref[j + 1, z, pl.ds(row, SUB), :]
    left = jnp.where(lane == LANES - 1, f_ref[j, z, pl.ds(row, SUB), :], f)
    right = jnp.where(lane == 0, f_ref[j + 2, z, pl.ds(row, SUB), :], f)
    return pltpu.roll(right, LANES - 1, 1) - pltpu.roll(left, 1, 1)


def rowwise(f_ref, j, z, row):
    return f_ref[j + 1, z, pl.ds(row + 1, SUB), :] - f_ref[j + 1, z, pl.ds(row - 1, SUB), :]


def march(f_ref, j, dst, shading, keep_first, keep_last, slices, rows):
    first = shading.base * keep_first, shading.slope * keep_first
    last = shading.base * keep_last, shading.slope * keep_last

    for top in range(0, rows, GROUP * SUB):
        starts = [TOP + top + SUB * r for r in range(GROUP)]

        def across(s0):
            return [sideways(f_ref, j, Z0 + s0 + u, row) for row in starts for u in range(UNROLL)]

        one = jnp.ones((SUB, LANES), jnp.float32)
        zero = jnp.zeros((SUB, LANES), jnp.float32)
        state = [[one, zero, zero, zero, zero] for _ in range(GROUP)]
        ahead = across(0)
        for s0 in range(0, slices, UNROLL):
            now = ahead
            if s0 + UNROLL < slices:
                ahead = across(s0 + UNROLL)
            for r, row in enumerate(starts):
                here = [f_ref[j + 1, Z0 + s0 + u - 1, pl.ds(row, SUB), :] for u in range(UNROLL + 2)]
                for u in range(UNROLL):
                    below, f, above = here[u], here[u + 1], here[u + 2]
                    dx = rowwise(f_ref, j, Z0 + s0 + u, row)
                    shade = shading.facing_and_norm(above - below, dx, now[r * UNROLL + u])
                    base, slope = shading.base, shading.slope
                    if s0 + u == 0:
                        base, slope = first
                    if s0 + u == slices - 1:
                        base, slope = last
                    f2 = f * f
                    t, m0, m1, m2, m3 = state[r]
                    behind = t * jnp.exp2(base + slope * f2)
                    w0 = (t - behind) * shade
                    w1 = w0 * f
                    state[r] = [behind, m0 + w0, m1 + w1, m2 + w0 * f2, m3 + w1 * f2]
        for r in range(GROUP):
            t, *moments = state[r]
            at = pl.ds(top + SUB * r, SUB)
            for c in range(3):
                dst[c, at, :] = shading.channel(c, *moments)
            dst[3, at, :] = t


def march_one(f_ref, j, z, dst, shading, in_front, rows):
    def tile(i, _):
        top = pl.multiple_of(i * SUB, SUB)
        row = top + TOP
        f = f_ref[j + 1, z, pl.ds(row, SUB), :]
        dz = f_ref[j + 1, z + 1, pl.ds(row, SUB), :] - f_ref[j + 1, z - 1, pl.ds(row, SUB), :]
        shade = shading.facing_and_norm(dz, rowwise(f_ref, j, z, row), sideways(f_ref, j, z, row))
        f2 = f * f
        passed = jnp.exp2(shading.base + shading.slope * f2)
        w0 = (1.0 - passed) * shade
        w1 = w0 * f
        at = pl.ds(top, SUB)
        seen = dst[3, at, :]
        one = jnp.ones_like(seen)
        old = jnp.where(in_front, passed, one)
        new = jnp.where(in_front, one, seen)
        for c in range(3):
            dst[c, at, :] = old * dst[c, at, :] + new * shading.channel(c, w0, w1, w0 * f2, w1 * f2)
        dst[3, at, :] = seen * passed
        return 0

    lax.fori_loop(0, rows // SUB, tile, 0)


def kernel(
    depths, tiles, slices, rows, blocks,
    field, absorb_in, color_in, light_in, out,
    f_ref, image, relay, frame, absorb, color, light,
    param_sem, load_sem, z_send, z_recv, e_send, e_recv, x_send, x_recv, y_send, y_recv,
    i_send, r_recv, i_recv, out_sem,
):
    d, t = lax.axis_index("depth"), lax.axis_index("tile")
    per = blocks // depths
    sent = (depths - 1) * per
    up_d, down_d = lax.rem(d + 1, depths), lax.rem(d + depths - 1, depths)
    next_t, prev_t = lax.rem(t + 1, tiles), lax.rem(t + tiles - 1, tiles)
    has_prev, has_next = t > 0, t < tiles - 1
    outer = jnp.logical_or(d == 0, d == depths - 1)

    params = [
        pltpu.make_async_copy(src, dst, param_sem.at[i])
        for i, (src, dst) in enumerate(((absorb_in, absorb), (color_in, color), (light_in, light)))
    ]

    def columns(j):
        return pl.ds(pl.multiple_of(j * LANES, LANES), LANES)

    def load(j):
        return pltpu.make_async_copy(
            field.at[:, :, columns(j)],
            f_ref.at[j + 1, pl.ds(Z0, slices), pl.ds(TOP, rows), :],
            load_sem.at[j],
        )

    barrier = pltpu.get_barrier_semaphore()
    for peer in ((up_d, t), (down_d, t), (d, next_t), (d, prev_t)):
        pl.semaphore_signal(barrier, inc=1, device_id=peer, device_id_type=MESH)
    for copy in params:
        copy.start()
    for j in range(blocks):
        load(j).start()

    zeros = jnp.zeros((SUB, LANES), jnp.float32)
    for edge in (0, blocks + 1):

        def clear(z, _):
            for row in range(0, rows, SUB):
                f_ref[edge, z, pl.ds(TOP + row, SUB), :] = zeros
            return 0

        lax.fori_loop(0, slices + 2 * Z0, clear, 0)
    for present, z, j0, j1 in (
        (d <= 1, Z0 - 1, 0, per),
        (d == 0, Z0 - 1, per, blocks),
        (d >= depths - 2, Z0 + slices, sent, blocks),
        (d == depths - 1, Z0 + slices, 0, sent),
    ):

        @pl.when(present)
        def _():
            def clear(j, _):
                for row in range(0, rows, SUB):
                    f_ref[j + 1, z, pl.ds(TOP + row, SUB), :] = zeros
                return 0

            lax.fori_loop(j0, j1, clear, 0)

    for present, row in ((has_prev, TOP - SUB), (has_next, TOP + rows)):

        @pl.when(jnp.logical_not(present))
        def _():
            def clear(j, _):
                for z in range(slices + 2 * Z0):
                    f_ref[j + 1, z, pl.ds(row, SUB), :] = zeros
                return 0

            lax.fori_loop(0, blocks, clear, 0)

    pl.semaphore_wait(barrier, 4)

    def order(me, s):
        far, own = s < per, s >= sent
        way = jnp.where(far, 0, jnp.where(own, 3, 1 + lax.rem(s, 2)))
        k = jnp.where(far, s, jnp.where(own, s - sent, (s - per) // 2))
        off = jnp.where(way == 0, 2, jnp.where(way == 1, 1, jnp.where(way == 2, depths - 1, 0)))
        return way, lax.rem(me + off, depths), k

    def block(me, s):
        _, owner, k = order(me, s)
        return owner * per + k

    def shifted(me, j):
        return j // per == jnp.where(me < depths // 2, 0, depths - 1)

    def sends_up(me, j):
        return jnp.logical_and(me < depths - 1, jnp.logical_not(jnp.logical_and(me == 0, shifted(me, j))))

    def sends_down(me, j):
        return jnp.logical_and(me > 0, jnp.logical_not(jnp.logical_and(me == depths - 1, shifted(me, j))))

    def z_copy(way, j):
        src, dst = ((slices - 1, Z0 - 1), (0, Z0 + slices))[way]
        return pltpu.make_async_remote_copy(
            src_ref=field.at[src, :, columns(j)],
            dst_ref=f_ref.at[j + 1, dst, pl.ds(TOP, rows), :],
            send_sem=z_send.at[way, j],
            recv_sem=z_recv.at[way, j],
            device_id=((up_d, down_d)[way], t),
            device_id_type=MESH,
        )

    def e_copy(k):
        up = d == depths - 2
        j = jnp.where(up, sent, 0) + k
        return pltpu.make_async_remote_copy(
            src_ref=field.at[jnp.where(up, slices - 2, 1), :, columns(j)],
            dst_ref=f_ref.at[j + 1, jnp.where(up, Z0 - 2, Z0 + slices + 1), pl.ds(TOP, rows), :],
            send_sem=e_send.at[k],
            recv_sem=e_recv.at[k],
            device_id=(jnp.where(up, up_d, down_d), t),
            device_id_type=MESH,
        )

    def e_wait(k):
        low = d == 0
        j = d * per + k
        pltpu.make_async_remote_copy(
            src_ref=field.at[0, :, columns(j)],
            dst_ref=f_ref.at[j + 1, jnp.where(low, Z0 + slices + 1, Z0 - 2), pl.ds(TOP, rows), :],
            send_sem=e_send.at[k],
            recv_sem=e_recv.at[k],
            device_id=(jnp.where(low, up_d, down_d), t),
            device_id_type=MESH,
        ).wait_recv()

    def x_copy(way, j):
        src, dst = ((rows - 1, TOP - 1), (0, TOP + rows))[way]
        return pltpu.make_async_remote_copy(
            src_ref=field.at[:, pl.ds(src, 1), columns(j)],
            dst_ref=f_ref.at[j + 1, pl.ds(Z0, slices), pl.ds(dst, 1), :],
            send_sem=x_send.at[way, j],
            recv_sem=x_recv.at[way, j],
            device_id=(d, (next_t, prev_t)[way]),
            device_id_type=MESH,
        )

    extra_z = jnp.where(d == 0, Z0 + slices, Z0 - 1)

    def y_copy(way, k):
        src, dst = ((TOP + rows - 1, TOP - 1), (TOP, TOP + rows))[way]
        j = d * per + k
        return pltpu.make_async_remote_copy(
            src_ref=f_ref.at[j + 1, extra_z, pl.ds(src, 1), :],
            dst_ref=f_ref.at[j + 1, extra_z, pl.ds(dst, 1), :],
            send_sem=y_send.at[way, k],
            recv_sem=y_recv.at[way, k],
            device_id=(d, (next_t, prev_t)[way]),
            device_id_type=MESH,
        )

    def start(s, _):
        j = block(up_d, s)

        @pl.when(sends_up(d, j))
        def _():
            z_copy(0, j).start()

        j = block(down_d, s)

        @pl.when(sends_down(d, j))
        def _():
            z_copy(1, j).start()

        j = block(d, s)

        @pl.when(has_next)
        def _():
            x_copy(0, j).start()

        @pl.when(has_prev)
        def _():
            x_copy(1, j).start()

        return 0

    lax.fori_loop(0, blocks, start, 0)

    @pl.when(jnp.logical_not(outer))
    def _():
        for k in range(per):
            e_copy(k).start()

    for copy in params:
        copy.wait()
    for j in range(blocks):
        load(j).wait()
    shading = Shading(absorb, color, light)

    def relays_up(me, k):
        inner = jnp.where(me == 1, k < SPLIT, k >= SPLIT)
        return jnp.logical_or(me == 0, jnp.logical_and(me < depths - 1, inner))

    def merges(way, k):
        from_below = jnp.logical_and(d > 0, relays_up(d - 1, k))
        from_above = jnp.logical_and(d < depths - 1, jnp.logical_not(relays_up(d + 1, k)))
        return jnp.logical_or(
            jnp.logical_and(way == 1, from_below), jnp.logical_and(way == 2, from_above)
        )

    def place(me, way, k):
        inner = jnp.where(way == 1, 0, jnp.where(way == 2, 2, 1))
        low = jnp.where(way == 1, 2, jnp.where(way == 2, 1, 0))
        high = jnp.where(way == 1, 1, jnp.where(way == 2, 0, 2))
        return sent + jnp.where(me == 0, low, jnp.where(me == depths - 1, high, inner)) * per + k

    def relay_copy(up, s, k):
        way = jnp.where(up, 0, 1)
        return pltpu.make_async_remote_copy(
            src_ref=image.at[s],
            dst_ref=relay.at[way, k],
            send_sem=i_send.at[s],
            recv_sem=r_recv.at[way, k],
            device_id=(jnp.where(up, up_d, down_d), t),
            device_id_type=MESH,
        )

    def image_copy(way, s, k):
        up = way == 1
        owner = jnp.where(up, up_d, down_d)
        return pltpu.make_async_remote_copy(
            src_ref=image.at[s],
            dst_ref=image.at[place(owner, way, k)],
            send_sem=i_send.at[s],
            recv_sem=i_recv.at[way - 1, k],
            device_id=(owner, t),
            device_id_type=MESH,
        )

    def merge(way, s, k):
        relay_copy(way == 1, s, k).wait_recv()
        front = way == 1

        def tile(i, _):
            at = pl.ds(pl.multiple_of(i * SUB, SUB), SUB)
            mine, other = image[s, 3, at, :], relay[way - 1, k, 3, at, :]
            one = jnp.ones_like(mine)
            a, b = jnp.where(front, other, one), jnp.where(front, one, mine)
            for c in range(3):
                image[s, c, at, :] = a * image[s, c, at, :] + b * relay[way - 1, k, c, at, :]
            image[s, 3, at, :] = mine * other
            return 0

        lax.fori_loop(0, rows // SUB, tile, 0)

    def step(s, _):
        way, owner, k = order(d, s)
        j = owner * per + k
        own = way == 3
        handed = jnp.logical_and(outer, own)

        @pl.when(jnp.logical_and(d > 0, jnp.logical_and(sends_up(d - 1, j), jnp.logical_not(handed))))
        def _():
            z_copy(0, j).wait_recv()

        @pl.when(jnp.logical_and(d < depths - 1, jnp.logical_and(sends_down(d + 1, j), jnp.logical_not(handed))))
        def _():
            z_copy(1, j).wait_recv()

        @pl.when(has_prev)
        def _():
            x_copy(0, j).wait_recv()

        @pl.when(has_next)
        def _():
            x_copy(1, j).wait_recv()

        @pl.when(jnp.logical_and(outer, s == sent - 2))
        def _():
            for i in range(per):

                @pl.when(d == 0)
                def _():
                    z_copy(1, d * per + i).wait_recv()

                @pl.when(d > 0)
                def _():
                    z_copy(0, d * per + i).wait_recv()

                @pl.when(has_next)
                def _():
                    y_copy(0, i).start()

                @pl.when(has_prev)
                def _():
                    y_copy(1, i).start()

        shift = shifted(d, j)
        keep_first = jnp.where(jnp.logical_and(d == 1, shift), 0.0, 1.0)
        keep_last = jnp.where(jnp.logical_and(d == depths - 2, shift), 0.0, 1.0)
        slot = jnp.where(own, place(d, 3, k), s)
        march(f_ref, j, image.at[slot], shading, keep_first, keep_last, slices, rows)

        @pl.when(way == 0)
        def _():
            relay_copy(relays_up(d, k), s, k).start()

        near = jnp.logical_or(way == 1, way == 2)

        @pl.when(jnp.logical_and(near, jnp.logical_not(merges(way, k))))
        def _():
            image_copy(way, s, k).start()

        late = jnp.maximum(s - LAG, 0)
        late_way, _, late_k = order(d, late)
        due = jnp.logical_and(s - LAG >= per, s - LAG < sent)

        @pl.when(jnp.logical_and(due, merges(late_way, late_k)))
        def _():
            merge(late_way, late, late_k)
            image_copy(late_way, late, late_k).start()

        @pl.when(handed)
        def _():
            e_wait(k)

            @pl.when(has_prev)
            def _():
                y_copy(0, k).wait_recv()

            @pl.when(has_next)
            def _():
                y_copy(1, k).wait_recv()

            march_one(f_ref, j, extra_z, image.at[slot], shading, d > 0, rows)

        return 0

    lax.fori_loop(0, blocks, step, 0)

    def finished(k):
        return pltpu.make_async_copy(frame.at[k], out.at[:, :, columns(k)], out_sem.at[k])

    for k in range(per):
        for way in (1, 2):
            pltpu.make_async_remote_copy(
                src_ref=image.at[0],
                dst_ref=image.at[place(d, way, k)],
                send_sem=i_send.at[0],
                recv_sem=i_recv.at[way - 1, k],
                device_id=(up_d, t),
                device_id_type=MESH,
            ).wait_recv()

        def compose(i, _):
            at = pl.ds(pl.multiple_of(i * SUB, SUB), SUB)
            seen = image[sent + k, 3, at, :]
            total = [image[sent + k, c, at, :] for c in range(3)]
            for q in (sent + per + k, sent + 2 * per + k):
                total = [total[c] + seen * image[q, c, at, :] for c in range(3)]
                seen = seen * image[q, 3, at, :]
            for c in range(3):
                frame[k, c, at, :] = total[c]
            frame[k, 3, at, :] = 1.0 - seen
            return 0

        lax.fori_loop(0, rows // SUB, compose, 0)
        finished(k).start()

    def drain(j, _):
        @pl.when(sends_up(d, j))
        def _():
            z_copy(0, j).wait_send()

        @pl.when(sends_down(d, j))
        def _():
            z_copy(1, j).wait_send()

        @pl.when(has_next)
        def _():
            x_copy(0, j).wait_send()

        @pl.when(has_prev)
        def _():
            x_copy(1, j).wait_send()

        return 0

    lax.fori_loop(0, blocks, drain, 0)

    def drain_images(s, _):
        relay_copy(d == 0, s, 0).wait_send()
        return 0

    lax.fori_loop(0, sent, drain_images, 0)

    for k in range(per):

        @pl.when(jnp.logical_not(outer))
        def _():
            e_copy(k).wait_send()

        @pl.when(jnp.logical_and(outer, has_next))
        def _():
            y_copy(0, k).wait_send()

        @pl.when(jnp.logical_and(outer, has_prev))
        def _():
            y_copy(1, k).wait_send()

    for k in range(per):
        finished(k).wait()


def on_device(depths, tiles, field, absorb, color, light):
    slices, rows, columns = field.shape
    blocks = columns // LANES
    per = blocks // depths
    sent = (depths - 1) * per
    dma = pltpu.SemaphoreType.DMA
    return pl.pallas_call(
        functools.partial(kernel, depths, tiles, slices, rows, blocks),
        out_shape=jax.ShapeDtypeStruct((4, rows, columns // depths), jnp.float32),
        in_specs=[pl.BlockSpec(memory_space=pl.ANY)] * 4,
        out_specs=pl.BlockSpec(memory_space=pl.ANY),
        scratch_shapes=[
            pltpu.VMEM((blocks + 2, slices + 2 * Z0, rows + 2 * TOP, LANES), jnp.float32),
            pltpu.VMEM((sent + 3 * per, 4, rows, LANES), jnp.float32),
            pltpu.VMEM((2, per, 4, rows, LANES), jnp.float32),
            pltpu.VMEM((per, 4, rows, LANES), jnp.float32),
            pltpu.SMEM((2,), jnp.float32),
            pltpu.SMEM((3, 4), jnp.float32),
            pltpu.SMEM((3,), jnp.float32),
            dma((3,)),
            dma((blocks,)),
            dma((2, blocks)),
            dma((2, blocks)),
            dma((per,)),
            dma((per,)),
            dma((2, blocks)),
            dma((2, blocks)),
            dma((2, per)),
            dma((2, per)),
            dma((sent,)),
            dma((2, per)),
            dma((2, per)),
            dma((per,)),
        ],
        compiler_params=pltpu.CompilerParams(
            collective_id=0, has_side_effects=True, vmem_limit_bytes=60 << 20
        ),
    )(field, absorb, color, light)


def solution(mesh):
    depths, tiles = mesh.shape["depth"], mesh.shape["tile"]
    return jax.shard_map(
        functools.partial(on_device, depths, tiles),
        mesh=mesh,
        in_specs=(P("depth", "tile", None), P(), P(), P()),
        out_specs=P(None, "tile", "depth"),
        check_vma=False,
    )
```

```python
import functools
import math

import jax
import jax.numpy as jnp
from jax import lax
from jax.experimental import pallas as pl
from jax.experimental.pallas import tpu as pltpu
from jax.sharding import PartitionSpec as P

MESH = pl.DeviceIdType.MESH
LANES = 128
SUB = 8
TOP = 8
Z0 = 2
GROUP = 2
UNROLL = 16
LAG = 4
SPLIT = 3


class Shading:
    def __init__(self, absorb, color, light):
        self.base = -absorb[0] * math.log2(math.e)
        self.slope = -absorb[1] * math.log2(math.e)
        self.light = light[0], light[1], light[2]
        self.color = color

    def facing_and_norm(self, dz, dx, dy):
        lz, lx, ly = self.light
        facing = jnp.abs(lz * dz + lx * dx + ly * dy)
        return facing * lax.rsqrt((dz * dz + 4.0) + (dx * dx + dy * dy))

    def channel(self, c, m0, m1, m2, m3):
        color = self.color
        return (color[c, 0] * m0 + color[c, 1] * m1) + (color[c, 2] * m2 + color[c, 3] * m3)


def sideways(f_ref, j, z, row):
    lane = lax.broadcasted_iota(jnp.int32, (SUB, LANES), 1)
    f = f_ref[j + 1, z, pl.ds(row, SUB), :]
    left = jnp.where(lane == LANES - 1, f_ref[j, z, pl.ds(row, SUB), :], f)
    right = jnp.where(lane == 0, f_ref[j + 2, z, pl.ds(row, SUB), :], f)
    return pltpu.roll(right, LANES - 1, 1) - pltpu.roll(left, 1, 1)


def rowwise(f_ref, j, z, row):
    return f_ref[j + 1, z, pl.ds(row + 1, SUB), :] - f_ref[j + 1, z, pl.ds(row - 1, SUB), :]


def march(f_ref, j, dst, shading, keep_first, keep_last, slices, rows):
    first = shading.base * keep_first, shading.slope * keep_first
    last = shading.base * keep_last, shading.slope * keep_last

    for top in range(0, rows, GROUP * SUB):
        starts = [TOP + top + SUB * r for r in range(GROUP)]

        def across(s0):
            return [sideways(f_ref, j, Z0 + s0 + u, row) for row in starts for u in range(UNROLL)]

        one = jnp.ones((SUB, LANES), jnp.float32)
        zero = jnp.zeros((SUB, LANES), jnp.float32)
        state = [[one, zero, zero, zero, zero] for _ in range(GROUP)]
        ahead = across(0)
        for s0 in range(0, slices, UNROLL):
            now = ahead
            if s0 + UNROLL < slices:
                ahead = across(s0 + UNROLL)
            for r, row in enumerate(starts):
                here = [f_ref[j + 1, Z0 + s0 + u - 1, pl.ds(row, SUB), :] for u in range(UNROLL + 2)]
                for u in range(UNROLL):
                    below, f, above = here[u], here[u + 1], here[u + 2]
                    dx = rowwise(f_ref, j, Z0 + s0 + u, row)
                    shade = shading.facing_and_norm(above - below, dx, now[r * UNROLL + u])
                    base, slope = shading.base, shading.slope
                    if s0 + u == 0:
                        base, slope = first
                    if s0 + u == slices - 1:
                        base, slope = last
                    f2 = f * f
                    t, m0, m1, m2, m3 = state[r]
                    behind = t * jnp.exp2(base + slope * f2)
                    w0 = (t - behind) * shade
                    w1 = w0 * f
                    state[r] = [behind, m0 + w0, m1 + w1, m2 + w0 * f2, m3 + w1 * f2]
        for r in range(GROUP):
            t, *moments = state[r]
            at = pl.ds(top + SUB * r, SUB)
            for c in range(3):
                dst[c, at, :] = shading.channel(c, *moments)
            dst[3, at, :] = t


def march_one(f_ref, j, z, dst, shading, in_front, rows):
    def tile(i, _):
        top = pl.multiple_of(i * SUB, SUB)
        row = top + TOP
        f = f_ref[j + 1, z, pl.ds(row, SUB), :]
        dz = f_ref[j + 1, z + 1, pl.ds(row, SUB), :] - f_ref[j + 1, z - 1, pl.ds(row, SUB), :]
        shade = shading.facing_and_norm(dz, rowwise(f_ref, j, z, row), sideways(f_ref, j, z, row))
        f2 = f * f
        passed = jnp.exp2(shading.base + shading.slope * f2)
        w0 = (1.0 - passed) * shade
        w1 = w0 * f
        at = pl.ds(top, SUB)
        seen = dst[3, at, :]
        one = jnp.ones_like(seen)
        old = jnp.where(in_front, passed, one)
        new = jnp.where(in_front, one, seen)
        for c in range(3):
            dst[c, at, :] = old * dst[c, at, :] + new * shading.channel(c, w0, w1, w0 * f2, w1 * f2)
        dst[3, at, :] = seen * passed
        return 0

    lax.fori_loop(0, rows // SUB, tile, 0)


def kernel(
    depths, tiles, slices, rows, blocks,
    field, absorb_in, color_in, light_in, out,
    f_ref, image, relay, absorb, color, light,
    param_sem, load_sem, z_send, z_recv, e_send, e_recv, x_send, x_recv, y_send, y_recv,
    i_send, r_recv, i_recv,
):
    d, t = lax.axis_index("depth"), lax.axis_index("tile")
    per = blocks // depths
    sent = (depths - 1) * per
    up_d, down_d = lax.rem(d + 1, depths), lax.rem(d + depths - 1, depths)
    next_t, prev_t = lax.rem(t + 1, tiles), lax.rem(t + tiles - 1, tiles)
    has_prev, has_next = t > 0, t < tiles - 1
    outer = jnp.logical_or(d == 0, d == depths - 1)

    params = [
        pltpu.make_async_copy(src, dst, param_sem.at[i])
        for i, (src, dst) in enumerate(((absorb_in, absorb), (color_in, color), (light_in, light)))
    ]

    def columns(j):
        return pl.ds(pl.multiple_of(j * LANES, LANES), LANES)

    def load(j):
        return pltpu.make_async_copy(
            field.at[:, :, columns(j)],
            f_ref.at[j + 1, pl.ds(Z0, slices), pl.ds(TOP, rows), :],
            load_sem.at[j],
        )

    barrier = pltpu.get_barrier_semaphore()
    for peer in (up_d, down_d):
        pl.semaphore_signal(barrier, inc=1, device_id=(peer, t), device_id_type=MESH)
    for present, peer in ((has_next, next_t), (has_prev, prev_t)):

        @pl.when(present)
        def _():
            pl.semaphore_signal(barrier, inc=1, device_id=(d, peer), device_id_type=MESH)

    for copy in params:
        copy.start()
    for j in range(blocks):
        load(j).start()

    zeros = jnp.zeros((SUB, LANES), jnp.float32)
    for edge in (0, blocks + 1):

        def clear(z, _):
            for row in range(0, rows, SUB):
                f_ref[edge, z, pl.ds(TOP + row, SUB), :] = zeros
            return 0

        lax.fori_loop(0, slices + 2 * Z0, clear, 0)
    for present, z, j0, j1 in (
        (d <= 1, Z0 - 1, 0, per),
        (d == 0, Z0 - 1, per, blocks),
        (d >= depths - 2, Z0 + slices, sent, blocks),
        (d == depths - 1, Z0 + slices, 0, sent),
    ):

        @pl.when(present)
        def _():
            def clear(j, _):
                for row in range(0, rows, SUB):
                    f_ref[j + 1, z, pl.ds(TOP + row, SUB), :] = zeros
                return 0

            lax.fori_loop(j0, j1, clear, 0)

    for present, row in ((has_prev, TOP - SUB), (has_next, TOP + rows)):

        @pl.when(jnp.logical_not(present))
        def _():
            def clear(j, _):
                for z in range(slices + 2 * Z0):
                    f_ref[j + 1, z, pl.ds(row, SUB), :] = zeros
                return 0

            lax.fori_loop(0, blocks, clear, 0)

    beside = has_prev.astype(jnp.int32) + has_next.astype(jnp.int32)
    pl.semaphore_wait(barrier, 2 + beside)

    def order(me, s):
        far, own = s < per, s >= sent
        way = jnp.where(far, 0, jnp.where(own, 3, 1 + lax.rem(s, 2)))
        k = jnp.where(far, s, jnp.where(own, s - sent, (s - per) // 2))
        off = jnp.where(way == 0, 2, jnp.where(way == 1, 1, jnp.where(way == 2, depths - 1, 0)))
        return way, lax.rem(me + off, depths), k

    def block(me, s):
        _, owner, k = order(me, s)
        return owner * per + k

    def shifted(me, j):
        return j // per == jnp.where(me < depths // 2, 0, depths - 1)

    def sends_up(me, j):
        return jnp.logical_and(me < depths - 1, jnp.logical_not(jnp.logical_and(me == 0, shifted(me, j))))

    def sends_down(me, j):
        return jnp.logical_and(me > 0, jnp.logical_not(jnp.logical_and(me == depths - 1, shifted(me, j))))

    def z_copy(way, j):
        src, dst = ((slices - 1, Z0 - 1), (0, Z0 + slices))[way]
        return pltpu.make_async_remote_copy(
            src_ref=field.at[src, :, columns(j)],
            dst_ref=f_ref.at[j + 1, dst, pl.ds(TOP, rows), :],
            send_sem=z_send.at[way, j],
            recv_sem=z_recv.at[way, j],
            device_id=((up_d, down_d)[way], t),
            device_id_type=MESH,
        )

    def e_copy(k):
        up = d == depths - 2
        j = jnp.where(up, sent, 0) + k
        return pltpu.make_async_remote_copy(
            src_ref=field.at[jnp.where(up, slices - 2, 1), :, columns(j)],
            dst_ref=f_ref.at[j + 1, jnp.where(up, Z0 - 2, Z0 + slices + 1), pl.ds(TOP, rows), :],
            send_sem=e_send.at[k],
            recv_sem=e_recv.at[k],
            device_id=(jnp.where(up, up_d, down_d), t),
            device_id_type=MESH,
        )

    def e_wait(k):
        low = d == 0
        j = d * per + k
        pltpu.make_async_remote_copy(
            src_ref=field.at[0, :, columns(j)],
            dst_ref=f_ref.at[j + 1, jnp.where(low, Z0 + slices + 1, Z0 - 2), pl.ds(TOP, rows), :],
            send_sem=e_send.at[k],
            recv_sem=e_recv.at[k],
            device_id=(jnp.where(low, up_d, down_d), t),
            device_id_type=MESH,
        ).wait_recv()

    def x_copy(way, j):
        src, dst = ((rows - 1, TOP - 1), (0, TOP + rows))[way]
        return pltpu.make_async_remote_copy(
            src_ref=field.at[:, pl.ds(src, 1), columns(j)],
            dst_ref=f_ref.at[j + 1, pl.ds(Z0, slices), pl.ds(dst, 1), :],
            send_sem=x_send.at[way, j],
            recv_sem=x_recv.at[way, j],
            device_id=(d, (next_t, prev_t)[way]),
            device_id_type=MESH,
        )

    extra_z = jnp.where(d == 0, Z0 + slices, Z0 - 1)

    def y_copy(way, k):
        src, dst = ((TOP + rows - 1, TOP - 1), (TOP, TOP + rows))[way]
        j = d * per + k
        return pltpu.make_async_remote_copy(
            src_ref=f_ref.at[j + 1, extra_z, pl.ds(src, 1), :],
            dst_ref=f_ref.at[j + 1, extra_z, pl.ds(dst, 1), :],
            send_sem=y_send.at[way, k],
            recv_sem=y_recv.at[way, k],
            device_id=(d, (next_t, prev_t)[way]),
            device_id_type=MESH,
        )

    def start(s, _):
        j = block(up_d, s)

        @pl.when(sends_up(d, j))
        def _():
            z_copy(0, j).start()

        j = block(down_d, s)

        @pl.when(sends_down(d, j))
        def _():
            z_copy(1, j).start()

        j = block(d, s)

        @pl.when(has_next)
        def _():
            x_copy(0, j).start()

        @pl.when(has_prev)
        def _():
            x_copy(1, j).start()

        return 0

    lax.fori_loop(0, blocks, start, 0)

    @pl.when(jnp.logical_not(outer))
    def _():
        for k in range(per):
            e_copy(k).start()

    for copy in params:
        copy.wait()
    for j in range(blocks):
        load(j).wait()
    shading = Shading(absorb, color, light)

    def relays_up(me, k):
        inner = jnp.where(me == 1, k < SPLIT, k >= SPLIT)
        return jnp.logical_or(me == 0, jnp.logical_and(me < depths - 1, inner))

    def merges(way, k):
        from_below = jnp.logical_and(d > 0, relays_up(d - 1, k))
        from_above = jnp.logical_and(d < depths - 1, jnp.logical_not(relays_up(d + 1, k)))
        return jnp.logical_or(
            jnp.logical_and(way == 1, from_below), jnp.logical_and(way == 2, from_above)
        )

    def place(me, way, k):
        inner = jnp.where(way == 1, 0, jnp.where(way == 2, 2, 1))
        low = jnp.where(way == 1, 2, jnp.where(way == 2, 1, 0))
        high = jnp.where(way == 1, 1, jnp.where(way == 2, 0, 2))
        return sent + jnp.where(me == 0, low, jnp.where(me == depths - 1, high, inner)) * per + k

    def relay_copy(up, s, k):
        way = jnp.where(up, 0, 1)
        return pltpu.make_async_remote_copy(
            src_ref=image.at[s],
            dst_ref=relay.at[way, k],
            send_sem=i_send.at[s],
            recv_sem=r_recv.at[way, k],
            device_id=(jnp.where(up, up_d, down_d), t),
            device_id_type=MESH,
        )

    def image_copy(way, s, k):
        up = way == 1
        owner = jnp.where(up, up_d, down_d)
        return pltpu.make_async_remote_copy(
            src_ref=image.at[s],
            dst_ref=image.at[place(owner, way, k)],
            send_sem=i_send.at[s],
            recv_sem=i_recv.at[way - 1, k],
            device_id=(owner, t),
            device_id_type=MESH,
        )

    def merge(way, s, k):
        relay_copy(way == 1, s, k).wait_recv()
        front = way == 1

        def tile(i, _):
            at = pl.ds(pl.multiple_of(i * SUB, SUB), SUB)
            mine, other = image[s, 3, at, :], relay[way - 1, k, 3, at, :]
            one = jnp.ones_like(mine)
            a, b = jnp.where(front, other, one), jnp.where(front, one, mine)
            for c in range(3):
                image[s, c, at, :] = a * image[s, c, at, :] + b * relay[way - 1, k, c, at, :]
            image[s, 3, at, :] = mine * other
            return 0

        lax.fori_loop(0, rows // SUB, tile, 0)

    def step(s, _):
        way, owner, k = order(d, s)
        j = owner * per + k
        own = way == 3
        handed = jnp.logical_and(outer, own)

        @pl.when(jnp.logical_and(d > 0, jnp.logical_and(sends_up(d - 1, j), jnp.logical_not(handed))))
        def _():
            z_copy(0, j).wait_recv()

        @pl.when(jnp.logical_and(d < depths - 1, jnp.logical_and(sends_down(d + 1, j), jnp.logical_not(handed))))
        def _():
            z_copy(1, j).wait_recv()

        @pl.when(has_prev)
        def _():
            x_copy(0, j).wait_recv()

        @pl.when(has_next)
        def _():
            x_copy(1, j).wait_recv()

        @pl.when(jnp.logical_and(outer, s == sent - 2))
        def _():
            for i in range(per):

                @pl.when(d == 0)
                def _():
                    z_copy(1, d * per + i).wait_recv()

                @pl.when(d > 0)
                def _():
                    z_copy(0, d * per + i).wait_recv()

                @pl.when(has_next)
                def _():
                    y_copy(0, i).start()

                @pl.when(has_prev)
                def _():
                    y_copy(1, i).start()

        shift = shifted(d, j)
        keep_first = jnp.where(jnp.logical_and(d == 1, shift), 0.0, 1.0)
        keep_last = jnp.where(jnp.logical_and(d == depths - 2, shift), 0.0, 1.0)
        slot = jnp.where(own, place(d, 3, k), s)
        march(f_ref, j, image.at[slot], shading, keep_first, keep_last, slices, rows)

        @pl.when(way == 0)
        def _():
            relay_copy(relays_up(d, k), s, k).start()

        near = jnp.logical_or(way == 1, way == 2)

        @pl.when(jnp.logical_and(near, jnp.logical_not(merges(way, k))))
        def _():
            image_copy(way, s, k).start()

        late = jnp.maximum(s - LAG, 0)
        late_way, _, late_k = order(d, late)
        due = jnp.logical_and(s - LAG >= per, s - LAG < sent)

        @pl.when(jnp.logical_and(due, merges(late_way, late_k)))
        def _():
            merge(late_way, late, late_k)
            image_copy(late_way, late, late_k).start()

        @pl.when(handed)
        def _():
            e_wait(k)

            @pl.when(has_prev)
            def _():
                y_copy(0, k).wait_recv()

            @pl.when(has_next)
            def _():
                y_copy(1, k).wait_recv()

            march_one(f_ref, j, extra_z, image.at[slot], shading, d > 0, rows)

        return 0

    lax.fori_loop(0, blocks, step, 0)

    for k in range(per):
        for way in (1, 2):
            pltpu.make_async_remote_copy(
                src_ref=image.at[0],
                dst_ref=image.at[place(d, way, k)],
                send_sem=i_send.at[0],
                recv_sem=i_recv.at[way - 1, k],
                device_id=(up_d, t),
                device_id_type=MESH,
            ).wait_recv()

        def compose(i, _):
            at = pl.ds(pl.multiple_of(i * SUB, SUB), SUB)
            seen = image[sent + k, 3, at, :]
            total = [image[sent + k, c, at, :] for c in range(3)]
            for q in (sent + per + k, sent + 2 * per + k):
                total = [total[c] + seen * image[q, c, at, :] for c in range(3)]
                seen = seen * image[q, 3, at, :]
            for c in range(3):
                out[c, at, k * LANES : (k + 1) * LANES] = total[c]
            out[3, at, k * LANES : (k + 1) * LANES] = 1.0 - seen
            return 0

        lax.fori_loop(0, rows // SUB, compose, 0)

    def drain(j, _):
        @pl.when(sends_up(d, j))
        def _():
            z_copy(0, j).wait_send()

        @pl.when(sends_down(d, j))
        def _():
            z_copy(1, j).wait_send()

        @pl.when(has_next)
        def _():
            x_copy(0, j).wait_send()

        @pl.when(has_prev)
        def _():
            x_copy(1, j).wait_send()

        return 0

    lax.fori_loop(0, blocks, drain, 0)

    def drain_images(s, _):
        relay_copy(d == 0, s, 0).wait_send()
        return 0

    lax.fori_loop(0, sent, drain_images, 0)

    for k in range(per):

        @pl.when(jnp.logical_not(outer))
        def _():
            e_copy(k).wait_send()

        @pl.when(jnp.logical_and(outer, has_next))
        def _():
            y_copy(0, k).wait_send()

        @pl.when(jnp.logical_and(outer, has_prev))
        def _():
            y_copy(1, k).wait_send()


def on_device(depths, tiles, field, absorb, color, light):
    slices, rows, columns = field.shape
    blocks = columns // LANES
    per = blocks // depths
    sent = (depths - 1) * per
    dma = pltpu.SemaphoreType.DMA
    return pl.pallas_call(
        functools.partial(kernel, depths, tiles, slices, rows, blocks),
        out_shape=pltpu.VMEM((4, rows, columns // depths), jnp.float32),
        in_specs=[pl.BlockSpec(memory_space=pl.ANY)] * 4,
        out_specs=pl.BlockSpec(memory_space=pltpu.VMEM),
        scratch_shapes=[
            pltpu.VMEM((blocks + 2, slices + 2 * Z0, rows + 2 * TOP, LANES), jnp.float32),
            pltpu.VMEM((sent + 3 * per, 4, rows, LANES), jnp.float32),
            pltpu.VMEM((2, per, 4, rows, LANES), jnp.float32),
            pltpu.SMEM((2,), jnp.float32),
            pltpu.SMEM((3, 4), jnp.float32),
            pltpu.SMEM((3,), jnp.float32),
            dma((3,)),
            dma((blocks,)),
            dma((2, blocks)),
            dma((2, blocks)),
            dma((per,)),
            dma((per,)),
            dma((2, blocks)),
            dma((2, blocks)),
            dma((2, per)),
            dma((2, per)),
            dma((sent,)),
            dma((2, per)),
            dma((2, per)),
        ],
        compiler_params=pltpu.CompilerParams(
            collective_id=0, has_side_effects=True, vmem_limit_bytes=55 << 20
        ),
    )(field, absorb, color, light)


def solution(mesh):
    depths, tiles = mesh.shape["depth"], mesh.shape["tile"]
    return jax.shard_map(
        functools.partial(on_device, depths, tiles),
        mesh=mesh,
        in_specs=(P("depth", "tile", None), P(), P(), P()),
        out_specs=P(None, "tile", "depth"),
        check_vma=False,
    )
```

```python
import functools
import math

import jax
import jax.numpy as jnp
from jax import lax
from jax.experimental import pallas as pl
from jax.experimental.pallas import tpu as pltpu
from jax.sharding import PartitionSpec as P

MESH = pl.DeviceIdType.MESH
LANES = 128
SUB = 8
TOP = 8
Z0 = 2
GROUP = 2
UNROLL = 16
LAG = 4
SPLIT = 2
CUT = 48


class Shading:
    def __init__(self, absorb, color, light):
        self.base = -absorb[0] * math.log2(math.e)
        self.slope = -absorb[1] * math.log2(math.e)
        self.light = light[0], light[1], light[2]
        self.color = color

    def facing_and_norm(self, dz, dx, dy):
        lz, lx, ly = self.light
        facing = jnp.abs(lz * dz + lx * dx + ly * dy)
        return facing * lax.rsqrt((dz * dz + 4.0) + (dx * dx + dy * dy))

    def channel(self, c, m0, m1, m2, m3):
        color = self.color
        return (color[c, 0] * m0 + color[c, 1] * m1) + (color[c, 2] * m2 + color[c, 3] * m3)


def sideways(f_ref, j, z, row):
    lane = lax.broadcasted_iota(jnp.int32, (SUB, LANES), 1)
    f = f_ref[j + 1, z, pl.ds(row, SUB), :]
    left = jnp.where(lane == LANES - 1, f_ref[j, z, pl.ds(row, SUB), :], f)
    right = jnp.where(lane == 0, f_ref[j + 2, z, pl.ds(row, SUB), :], f)
    return pltpu.roll(right, LANES - 1, 1) - pltpu.roll(left, 1, 1)


def rowwise(f_ref, j, z, row):
    return f_ref[j + 1, z, pl.ds(row + 1, SUB), :] - f_ref[j + 1, z, pl.ds(row - 1, SUB), :]


def march(f_ref, j, dst, shading, keep_first, keep_last, slices, rows):
    first = shading.base * keep_first, shading.slope * keep_first
    last = shading.base * keep_last, shading.slope * keep_last

    for top in range(0, rows, GROUP * SUB):
        starts = [TOP + top + SUB * r for r in range(GROUP)]

        def across(s0):
            return [sideways(f_ref, j, Z0 + s0 + u, row) for row in starts for u in range(UNROLL)]

        one = jnp.ones((SUB, LANES), jnp.float32)
        zero = jnp.zeros((SUB, LANES), jnp.float32)
        state = [[one, zero, zero, zero, zero] for _ in range(GROUP)]
        ahead = across(0)
        for s0 in range(0, slices, UNROLL):
            now = ahead
            if s0 + UNROLL < slices:
                ahead = across(s0 + UNROLL)
            for r, row in enumerate(starts):
                here = [f_ref[j + 1, Z0 + s0 + u - 1, pl.ds(row, SUB), :] for u in range(UNROLL + 2)]
                for u in range(UNROLL):
                    below, f, above = here[u], here[u + 1], here[u + 2]
                    dx = rowwise(f_ref, j, Z0 + s0 + u, row)
                    shade = shading.facing_and_norm(above - below, dx, now[r * UNROLL + u])
                    base, slope = shading.base, shading.slope
                    if s0 + u == 0:
                        base, slope = first
                    if s0 + u == slices - 1:
                        base, slope = last
                    f2 = f * f
                    t, m0, m1, m2, m3 = state[r]
                    behind = t * jnp.exp2(base + slope * f2)
                    w0 = (t - behind) * shade
                    w1 = w0 * f
                    state[r] = [behind, m0 + w0, m1 + w1, m2 + w0 * f2, m3 + w1 * f2]
        for r in range(GROUP):
            t, *moments = state[r]
            at = pl.ds(top + SUB * r, SUB)
            for c in range(3):
                dst[c, at, :] = shading.channel(c, *moments)
            dst[3, at, :] = t


def march_one(f_ref, j, z, dst, shading, in_front, rows):
    def tile(top):
        row = top + TOP
        f = f_ref[j + 1, z, pl.ds(row, SUB), :]
        dz = f_ref[j + 1, z + 1, pl.ds(row, SUB), :] - f_ref[j + 1, z - 1, pl.ds(row, SUB), :]
        shade = shading.facing_and_norm(dz, rowwise(f_ref, j, z, row), sideways(f_ref, j, z, row))
        f2 = f * f
        passed = jnp.exp2(shading.base + shading.slope * f2)
        w0 = (1.0 - passed) * shade
        w1 = w0 * f
        at = pl.ds(top, SUB)
        seen = dst[3, at, :]
        one = jnp.ones_like(seen)
        old = jnp.where(in_front, passed, one)
        new = jnp.where(in_front, one, seen)
        for c in range(3):
            dst[c, at, :] = old * dst[c, at, :] + new * shading.channel(c, w0, w1, w0 * f2, w1 * f2)
        dst[3, at, :] = seen * passed

    for top in range(0, rows, SUB):
        tile(top)


def kernel(
    depths, tiles, slices, rows, blocks,
    field, absorb_in, color_in, light_in, out,
    f_ref, image, relay, absorb, color, light,
    param_sem, load_sem, z_send, z_recv, e_send, e_recv, x_send, x_recv, y_send, y_recv,
    i_send, r_recv, i_recv,
):
    d, t = lax.axis_index("depth"), lax.axis_index("tile")
    per = blocks // depths
    sent = (depths - 1) * per
    up_d, down_d = lax.rem(d + 1, depths), lax.rem(d + depths - 1, depths)
    next_t, prev_t = lax.rem(t + 1, tiles), lax.rem(t + tiles - 1, tiles)
    has_prev, has_next = t > 0, t < tiles - 1
    outer = jnp.logical_or(d == 0, d == depths - 1)

    params = [
        pltpu.make_async_copy(src, dst, param_sem.at[i])
        for i, (src, dst) in enumerate(((absorb_in, absorb), (color_in, color), (light_in, light)))
    ]

    def columns(j):
        return pl.ds(pl.multiple_of(j * LANES, LANES), LANES)

    def load(j):
        return pltpu.make_async_copy(
            field.at[:, :, columns(j)],
            f_ref.at[j + 1, pl.ds(Z0, slices), pl.ds(TOP, rows), :],
            load_sem.at[j],
        )

    barrier = pltpu.get_barrier_semaphore()
    for peer in (up_d, down_d):
        pl.semaphore_signal(barrier, inc=1, device_id=(peer, t), device_id_type=MESH)
    for present, peer in ((has_next, next_t), (has_prev, prev_t)):

        @pl.when(present)
        def _():
            pl.semaphore_signal(barrier, inc=1, device_id=(d, peer), device_id_type=MESH)

    for copy in params:
        copy.start()
    for j in range(blocks):
        load(j).start()

    zeros = jnp.zeros((SUB, LANES), jnp.float32)
    for edge in (0, blocks + 1):

        def clear(z, _):
            for row in range(0, rows, SUB):
                f_ref[edge, z, pl.ds(TOP + row, SUB), :] = zeros
            return 0

        lax.fori_loop(0, slices + 2 * Z0, clear, 0)
    for present, z, j0, j1 in (
        (d == 0, Z0 - 1, 0, blocks),
        (d == 1, Z0 - 1, 0, per),
        (d == 1, Z0 - 1, 2 * per - 1, 2 * per),
        (d == depths - 2, Z0 + slices, sent - 1, blocks),
        (d == depths - 1, Z0 + slices, 0, blocks),
    ):

        @pl.when(present)
        def _():
            def clear(j, _):
                for row in range(0, rows, SUB):
                    f_ref[j + 1, z, pl.ds(TOP + row, SUB), :] = zeros
                return 0

            lax.fori_loop(j0, j1, clear, 0)

    for present, row in ((has_prev, TOP - SUB), (has_next, TOP + rows)):

        @pl.when(jnp.logical_not(present))
        def _():
            def clear(j, _):
                for z in range(slices + 2 * Z0):
                    f_ref[j + 1, z, pl.ds(row, SUB), :] = zeros
                return 0

            lax.fori_loop(0, blocks, clear, 0)

    beside = has_prev.astype(jnp.int32) + has_next.astype(jnp.int32)
    pl.semaphore_wait(barrier, 2 + beside)

    def order(me, s):
        far, own = s < per, s >= sent
        way = jnp.where(far, 0, jnp.where(own, 3, 1 + lax.rem(s, 2)))
        k = jnp.where(far, s, jnp.where(own, s - sent, (s - per) // 2))
        off = jnp.where(way == 0, 2, jnp.where(way == 1, 1, jnp.where(way == 2, depths - 1, 0)))
        return way, lax.rem(me + off, depths), k

    def block(me, s):
        _, owner, k = order(me, s)
        return owner * per + k

    def shifted(me, j):
        low = jnp.logical_or(j < per, j == 2 * per - 1)
        return jnp.where(me < depths // 2, low, j >= sent - 1)

    def taken(high, i):
        return jnp.where(high, sent - 1 + i, jnp.where(i < per, i, 2 * per - 1))

    def sends_up(me, j):
        return jnp.logical_and(me < depths - 1, jnp.logical_not(jnp.logical_and(me == 0, shifted(me, j))))

    def sends_down(me, j):
        return jnp.logical_and(me > 0, jnp.logical_not(jnp.logical_and(me == depths - 1, shifted(me, j))))

    def z_copy(way, j):
        src, dst = ((slices - 1, Z0 - 1), (0, Z0 + slices))[way]
        return pltpu.make_async_remote_copy(
            src_ref=field.at[src, :, columns(j)],
            dst_ref=f_ref.at[j + 1, dst, pl.ds(TOP, rows), :],
            send_sem=z_send.at[way, j],
            recv_sem=z_recv.at[way, j],
            device_id=((up_d, down_d)[way], t),
            device_id_type=MESH,
        )

    def e_copy(k):
        up = d == depths - 2
        j = taken(up, k)
        return pltpu.make_async_remote_copy(
            src_ref=field.at[jnp.where(up, slices - 2, 1), :, columns(j)],
            dst_ref=f_ref.at[j + 1, jnp.where(up, Z0 - 2, Z0 + slices + 1), pl.ds(TOP, rows), :],
            send_sem=e_send.at[k],
            recv_sem=e_recv.at[k],
            device_id=(jnp.where(up, up_d, down_d), t),
            device_id_type=MESH,
        )

    def e_wait(k):
        low = d == 0
        j = taken(d > 0, k)
        pltpu.make_async_remote_copy(
            src_ref=field.at[0, :, columns(j)],
            dst_ref=f_ref.at[j + 1, jnp.where(low, Z0 + slices + 1, Z0 - 2), pl.ds(TOP, rows), :],
            send_sem=e_send.at[k],
            recv_sem=e_recv.at[k],
            device_id=(jnp.where(low, up_d, down_d), t),
            device_id_type=MESH,
        ).wait_recv()

    def x_copy(way, j):
        src, dst = ((rows - 1, TOP - 1), (0, TOP + rows))[way]
        return pltpu.make_async_remote_copy(
            src_ref=field.at[:, pl.ds(src, 1), columns(j)],
            dst_ref=f_ref.at[j + 1, pl.ds(Z0, slices), pl.ds(dst, 1), :],
            send_sem=x_send.at[way, j],
            recv_sem=x_recv.at[way, j],
            device_id=(d, (next_t, prev_t)[way]),
            device_id_type=MESH,
        )

    extra_z = jnp.where(d == 0, Z0 + slices, Z0 - 1)

    def y_copy(way, k):
        src, dst = ((TOP + rows - 1, TOP - 1), (TOP, TOP + rows))[way]
        j = taken(d > 0, k)
        return pltpu.make_async_remote_copy(
            src_ref=f_ref.at[j + 1, extra_z, pl.ds(src, 1), :],
            dst_ref=f_ref.at[j + 1, extra_z, pl.ds(dst, 1), :],
            send_sem=y_send.at[way, k],
            recv_sem=y_recv.at[way, k],
            device_id=(d, (next_t, prev_t)[way]),
            device_id_type=MESH,
        )

    def start(s, _):
        j = block(up_d, s)

        @pl.when(sends_up(d, j))
        def _():
            z_copy(0, j).start()

        j = block(down_d, s)

        @pl.when(sends_down(d, j))
        def _():
            z_copy(1, j).start()

        j = block(d, s)

        @pl.when(has_next)
        def _():
            x_copy(0, j).start()

        @pl.when(has_prev)
        def _():
            x_copy(1, j).start()

        return 0

    lax.fori_loop(0, blocks, start, 0)

    @pl.when(jnp.logical_not(outer))
    def _():
        for k in range(per + 1):
            e_copy(k).start()

    for copy in params:
        copy.wait()
    for j in range(blocks):
        load(j).wait()
    shading = Shading(absorb, color, light)

    def relays_up(me, k, part):
        through = jnp.logical_or(k < SPLIT, jnp.logical_and(k == SPLIT, part == 0))
        inner = jnp.where(me == 1, through, jnp.logical_not(through))
        return jnp.logical_or(me == 0, jnp.logical_and(me < depths - 1, inner))

    def merges(way, k, part):
        from_below = jnp.logical_and(d > 0, relays_up(d - 1, k, part))
        from_above = jnp.logical_and(d < depths - 1, jnp.logical_not(relays_up(d + 1, k, part)))
        return jnp.logical_or(
            jnp.logical_and(way == 1, from_below), jnp.logical_and(way == 2, from_above)
        )

    def merges_any(way, k):
        return jnp.logical_or(merges(way, k, 0), merges(way, k, 1))

    def place(me, way, k):
        inner = jnp.where(way == 1, 0, jnp.where(way == 2, 2, 1))
        low = jnp.where(way == 1, 2, jnp.where(way == 2, 1, 0))
        high = jnp.where(way == 1, 1, jnp.where(way == 2, 0, 2))
        return sent + jnp.where(me == 0, low, jnp.where(me == depths - 1, high, inner)) * per + k

    parts = ((0, CUT), (CUT, rows - CUT))

    def relay_copy(up, s, k, part):
        way = jnp.where(up, 0, 1)
        at = pl.ds(*parts[part])
        return pltpu.make_async_remote_copy(
            src_ref=image.at[s, :, at, :],
            dst_ref=relay.at[way, k, :, at, :],
            send_sem=i_send.at[part, s],
            recv_sem=r_recv.at[way, k, part],
            device_id=(jnp.where(up, up_d, down_d), t),
            device_id_type=MESH,
        )

    def image_copy(way, s, k):
        up = way == 1
        owner = jnp.where(up, up_d, down_d)
        return pltpu.make_async_remote_copy(
            src_ref=image.at[s],
            dst_ref=image.at[place(owner, way, k)],
            send_sem=i_send.at[0, s],
            recv_sem=i_recv.at[way - 1, k],
            device_id=(owner, t),
            device_id_type=MESH,
        )

    def merge(way, s, k, part):
        relay_copy(way == 1, s, k, part).wait_recv()
        front = way == 1
        top, count = parts[part]
        for row in range(top, top + count, SUB):
            at = pl.ds(row, SUB)
            mine, other = image[s, 3, at, :], relay[way - 1, k, 3, at, :]
            one = jnp.ones_like(mine)
            a, b = jnp.where(front, other, one), jnp.where(front, one, mine)
            for c in range(3):
                image[s, c, at, :] = a * image[s, c, at, :] + b * relay[way - 1, k, c, at, :]
            image[s, 3, at, :] = mine * other

    def step(s, _):
        way, owner, k = order(d, s)
        j = owner * per + k
        own = way == 3
        shift = shifted(d, j)
        handed = jnp.logical_and(outer, shift)
        waited = jnp.logical_and(outer, own)

        @pl.when(jnp.logical_and(d > 0, jnp.logical_and(sends_up(d - 1, j), jnp.logical_not(waited))))
        def _():
            z_copy(0, j).wait_recv()

        @pl.when(jnp.logical_and(d < depths - 1, jnp.logical_and(sends_down(d + 1, j), jnp.logical_not(waited))))
        def _():
            z_copy(1, j).wait_recv()

        @pl.when(has_prev)
        def _():
            x_copy(0, j).wait_recv()

        @pl.when(has_next)
        def _():
            x_copy(1, j).wait_recv()

        @pl.when(jnp.logical_and(outer, s == sent))
        def _():
            for i in range(per):

                @pl.when(d == 0)
                def _():
                    z_copy(1, d * per + i).wait_recv()

                @pl.when(d > 0)
                def _():
                    z_copy(0, d * per + i).wait_recv()

            for i in range(per + 1):

                @pl.when(has_next)
                def _():
                    y_copy(0, i).start()

                @pl.when(has_prev)
                def _():
                    y_copy(1, i).start()

        keep_first = jnp.where(jnp.logical_and(d == 1, shift), 0.0, 1.0)
        keep_last = jnp.where(jnp.logical_and(d == depths - 2, shift), 0.0, 1.0)
        slot = jnp.where(own, place(d, 3, k), s)
        march(f_ref, j, image.at[slot], shading, keep_first, keep_last, slices, rows)

        @pl.when(way == 0)
        def _():
            for part in range(2):
                relay_copy(relays_up(d, k, part), s, k, part).start()

        near = jnp.logical_or(way == 1, way == 2)

        @pl.when(jnp.logical_and(near, jnp.logical_not(jnp.logical_or(handed, merges_any(way, k)))))
        def _():
            image_copy(way, s, k).start()

        late = jnp.maximum(s - LAG, 0)
        late_way, _, late_k = order(d, late)
        due = jnp.logical_and(s - LAG >= per, s - LAG < sent)

        for part in range(2):

            @pl.when(jnp.logical_and(due, merges(late_way, late_k, part)))
            def _():
                merge(late_way, late, late_k, part)

        @pl.when(jnp.logical_and(due, merges_any(late_way, late_k)))
        def _():
            image_copy(late_way, late, late_k).start()

        return 0

    lax.fori_loop(0, blocks, step, 0)

    @pl.when(outer)
    def _():
        def complete(n, _):
            i = jnp.where(d > 0, n, lax.rem(n + per, per + 1))
            j = taken(d > 0, i)
            e_wait(i)

            @pl.when(has_prev)
            def _():
                y_copy(0, i).wait_recv()

            @pl.when(has_next)
            def _():
                y_copy(1, i).wait_recv()

            away = n == 0
            s = jnp.where(d > 0, sent - 1, sent - 2)
            slot = jnp.where(away, s, place(d, 3, n - 1))
            march_one(f_ref, j, extra_z, image.at[slot], shading, d > 0, rows)

            @pl.when(away)
            def _():
                image_copy(jnp.where(d > 0, 2, 1), s, per - 1).start()

            return 0

        lax.fori_loop(0, per + 1, complete, 0)

    def drain(j, _):
        @pl.when(sends_up(d, j))
        def _():
            z_copy(0, j).wait_send()

        @pl.when(sends_down(d, j))
        def _():
            z_copy(1, j).wait_send()

        @pl.when(has_next)
        def _():
            x_copy(0, j).wait_send()

        @pl.when(has_prev)
        def _():
            x_copy(1, j).wait_send()

        return 0

    lax.fori_loop(0, blocks, drain, 0)

    for k in range(per + 1):

        @pl.when(jnp.logical_not(outer))
        def _():
            e_copy(k).wait_send()

        @pl.when(jnp.logical_and(outer, has_next))
        def _():
            y_copy(0, k).wait_send()

        @pl.when(jnp.logical_and(outer, has_prev))
        def _():
            y_copy(1, k).wait_send()

    def compose(k, _):
        for way in (1, 2):
            pltpu.make_async_remote_copy(
                src_ref=image.at[0],
                dst_ref=image.at[place(d, way, k)],
                send_sem=i_send.at[0, 0],
                recv_sem=i_recv.at[way - 1, k],
                device_id=(up_d, t),
                device_id_type=MESH,
            ).wait_recv()
        for top in range(0, rows, SUB):
            at = pl.ds(top, SUB)
            seen = image[sent + k, 3, at, :]
            total = [image[sent + k, c, at, :] for c in range(3)]
            for q in (sent + per + k, sent + 2 * per + k):
                total = [total[c] + seen * image[q, c, at, :] for c in range(3)]
                seen = seen * image[q, 3, at, :]
            for c in range(3):
                out[c, at, columns(k)] = total[c]
            out[3, at, columns(k)] = 1.0 - seen
        return 0

    lax.fori_loop(0, per, compose, 0)

    for s in range(sent):
        if s < per:
            for part in range(2):
                relay_copy(d == 0, s, 0, part).wait_send()
        else:
            image_copy(jnp.where(d >= 0, 1, 2), s, 0).wait_send()


def on_device(depths, tiles, field, absorb, color, light):
    slices, rows, columns = field.shape
    blocks = columns // LANES
    per = blocks // depths
    sent = (depths - 1) * per
    dma = pltpu.SemaphoreType.DMA
    return pl.pallas_call(
        functools.partial(kernel, depths, tiles, slices, rows, blocks),
        out_shape=pltpu.VMEM((4, rows, columns // depths), jnp.float32),
        in_specs=[pl.BlockSpec(memory_space=pl.ANY)] * 4,
        out_specs=pl.BlockSpec(memory_space=pltpu.VMEM),
        scratch_shapes=[
            pltpu.VMEM((blocks + 2, slices + 2 * Z0, rows + 2 * TOP, LANES), jnp.float32),
            pltpu.VMEM((sent + 3 * per, 4, rows, LANES), jnp.float32),
            pltpu.VMEM((2, per, 4, rows, LANES), jnp.float32),
            pltpu.SMEM((2,), jnp.float32),
            pltpu.SMEM((3, 4), jnp.float32),
            pltpu.SMEM((3,), jnp.float32),
            dma((3,)),
            dma((blocks,)),
            dma((2, blocks)),
            dma((2, blocks)),
            dma((per + 1,)),
            dma((per + 1,)),
            dma((2, blocks)),
            dma((2, blocks)),
            dma((2, per + 1)),
            dma((2, per + 1)),
            dma((2, sent)),
            dma((2, per, 2)),
            dma((2, per)),
        ],
        compiler_params=pltpu.CompilerParams(
            collective_id=0, has_side_effects=True, vmem_limit_bytes=55 << 20
        ),
    )(field, absorb, color, light)


def solution(mesh):
    depths, tiles = mesh.shape["depth"], mesh.shape["tile"]
    return jax.shard_map(
        functools.partial(on_device, depths, tiles),
        mesh=mesh,
        in_specs=(P("depth", "tile", None), P(), P(), P()),
        out_specs=P(None, "tile", "depth"),
        check_vma=False,
    )
```

```python
import functools
import math

import jax
import jax.numpy as jnp
from jax import lax
from jax.experimental import pallas as pl
from jax.experimental.pallas import tpu as pltpu
from jax.sharding import PartitionSpec as P

MESH = pl.DeviceIdType.MESH
LANES = 128
SUB = 8
TOP = 8
Z0 = 2
GROUP = 2
UNROLL = 16
LAG = 4
SPLIT = 2
CUT = 48


class Shading:
    def __init__(self, absorb, color, light):
        self.base = -absorb[0] * math.log2(math.e)
        self.slope = -absorb[1] * math.log2(math.e)
        self.light = light[0], light[1], light[2]
        self.color = color

    def facing_and_norm(self, dz, dx, dy):
        lz, lx, ly = self.light
        facing = jnp.abs(lz * dz + lx * dx + ly * dy)
        return facing * lax.rsqrt((dz * dz + 4.0) + (dx * dx + dy * dy))

    def channel(self, c, m0, m1, m2, m3):
        color = self.color
        return (color[c, 0] * m0 + color[c, 1] * m1) + (color[c, 2] * m2 + color[c, 3] * m3)


def sideways(f_ref, j, z, row):
    lane = lax.broadcasted_iota(jnp.int32, (SUB, LANES), 1)
    f = f_ref[j + 1, z, pl.ds(row, SUB), :]
    left = jnp.where(lane == LANES - 1, f_ref[j, z, pl.ds(row, SUB), :], f)
    right = jnp.where(lane == 0, f_ref[j + 2, z, pl.ds(row, SUB), :], f)
    return pltpu.roll(right, LANES - 1, 1) - pltpu.roll(left, 1, 1)


def rowwise(f_ref, j, z, row):
    return f_ref[j + 1, z, pl.ds(row + 1, SUB), :] - f_ref[j + 1, z, pl.ds(row - 1, SUB), :]


def march(f_ref, j, dst, shading, keep_first, keep_last, slices, rows):
    first = shading.base * keep_first, shading.slope * keep_first
    last = shading.base * keep_last, shading.slope * keep_last

    for top in range(0, rows, GROUP * SUB):
        starts = [TOP + top + SUB * r for r in range(GROUP)]

        def across(s0):
            return [sideways(f_ref, j, Z0 + s0 + u, row) for row in starts for u in range(UNROLL)]

        one = jnp.ones((SUB, LANES), jnp.float32)
        zero = jnp.zeros((SUB, LANES), jnp.float32)
        state = [[one, zero, zero, zero, zero] for _ in range(GROUP)]
        ahead = across(0)
        for s0 in range(0, slices, UNROLL):
            now = ahead
            if s0 + UNROLL < slices:
                ahead = across(s0 + UNROLL)
            for r, row in enumerate(starts):
                here = [f_ref[j + 1, Z0 + s0 + u - 1, pl.ds(row, SUB), :] for u in range(UNROLL + 2)]
                for u in range(UNROLL):
                    below, f, above = here[u], here[u + 1], here[u + 2]
                    dx = rowwise(f_ref, j, Z0 + s0 + u, row)
                    shade = shading.facing_and_norm(above - below, dx, now[r * UNROLL + u])
                    base, slope = shading.base, shading.slope
                    if s0 + u == 0:
                        base, slope = first
                    if s0 + u == slices - 1:
                        base, slope = last
                    f2 = f * f
                    t, m0, m1, m2, m3 = state[r]
                    behind = t * jnp.exp2(base + slope * f2)
                    w0 = (t - behind) * shade
                    w1 = w0 * f
                    state[r] = [behind, m0 + w0, m1 + w1, m2 + w0 * f2, m3 + w1 * f2]
        for r in range(GROUP):
            t, *moments = state[r]
            at = pl.ds(top + SUB * r, SUB)
            for c in range(3):
                dst[c, at, :] = shading.channel(c, *moments)
            dst[3, at, :] = t


def march_one(f_ref, j, z, dst, shading, in_front, rows):
    def tile(top):
        row = top + TOP
        f = f_ref[j + 1, z, pl.ds(row, SUB), :]
        dz = f_ref[j + 1, z + 1, pl.ds(row, SUB), :] - f_ref[j + 1, z - 1, pl.ds(row, SUB), :]
        shade = shading.facing_and_norm(dz, rowwise(f_ref, j, z, row), sideways(f_ref, j, z, row))
        f2 = f * f
        passed = jnp.exp2(shading.base + shading.slope * f2)
        w0 = (1.0 - passed) * shade
        w1 = w0 * f
        at = pl.ds(top, SUB)
        seen = dst[3, at, :]
        one = jnp.ones_like(seen)
        old = jnp.where(in_front, passed, one)
        new = jnp.where(in_front, one, seen)
        for c in range(3):
            dst[c, at, :] = old * dst[c, at, :] + new * shading.channel(c, w0, w1, w0 * f2, w1 * f2)
        dst[3, at, :] = seen * passed

    for top in range(0, rows, SUB):
        tile(top)


def kernel(
    depths, tiles, slices, rows, blocks,
    field, absorb_in, color_in, light_in, out,
    f_ref, image, relay, absorb, color, light,
    param_sem, load_sem, z_send, z_recv, e_send, e_recv, x_send, x_recv, y_send, y_recv,
    i_send, r_recv, i_recv,
):
    d, t = lax.axis_index("depth"), lax.axis_index("tile")
    per = blocks // depths
    sent = (depths - 1) * per
    up_d, down_d = lax.rem(d + 1, depths), lax.rem(d + depths - 1, depths)
    next_t, prev_t = lax.rem(t + 1, tiles), lax.rem(t + tiles - 1, tiles)
    has_prev, has_next = t > 0, t < tiles - 1
    outer = jnp.logical_or(d == 0, d == depths - 1)

    params = [
        pltpu.make_async_copy(src, dst, param_sem.at[i])
        for i, (src, dst) in enumerate(((absorb_in, absorb), (color_in, color), (light_in, light)))
    ]

    def columns(j):
        return pl.ds(pl.multiple_of(j * LANES, LANES), LANES)

    def load(j):
        return pltpu.make_async_copy(
            field.at[:, :, columns(j)],
            f_ref.at[j + 1, pl.ds(Z0, slices), pl.ds(TOP, rows), :],
            load_sem.at[j],
        )

    barrier = pltpu.get_barrier_semaphore()
    for peer in (up_d, down_d):
        pl.semaphore_signal(barrier, inc=1, device_id=(peer, t), device_id_type=MESH)
    for present, peer in ((has_next, next_t), (has_prev, prev_t)):

        @pl.when(present)
        def _():
            pl.semaphore_signal(barrier, inc=1, device_id=(d, peer), device_id_type=MESH)

    for copy in params:
        copy.start()
    for j in range(blocks):
        load(j).start()

    beside = has_prev.astype(jnp.int32) + has_next.astype(jnp.int32)
    pl.semaphore_wait(barrier, 2 + beside)

    def order(me, s):
        far, own = s < per, s >= sent
        way = jnp.where(far, 0, jnp.where(own, 3, 1 + lax.rem(s, 2)))
        k = jnp.where(far, s, jnp.where(own, s - sent, (s - per) // 2))
        off = jnp.where(way == 0, 2, jnp.where(way == 1, 1, jnp.where(way == 2, depths - 1, 0)))
        return way, lax.rem(me + off, depths), k

    def block(me, s):
        _, owner, k = order(me, s)
        return owner * per + k

    def shifted(me, j):
        low = jnp.logical_or(j < per, j == 2 * per - 1)
        return jnp.where(me < depths // 2, low, j >= sent - 1)

    def taken(high, i):
        return jnp.where(high, sent - 1 + i, jnp.where(i < per, i, 2 * per - 1))

    def sends_up(me, j):
        return jnp.logical_and(me < depths - 1, jnp.logical_not(jnp.logical_and(me == 0, shifted(me, j))))

    def sends_down(me, j):
        return jnp.logical_and(me > 0, jnp.logical_not(jnp.logical_and(me == depths - 1, shifted(me, j))))

    def z_copy(way, j):
        src, dst = ((slices - 1, Z0 - 1), (0, Z0 + slices))[way]
        return pltpu.make_async_remote_copy(
            src_ref=field.at[src, :, columns(j)],
            dst_ref=f_ref.at[j + 1, dst, pl.ds(TOP, rows), :],
            send_sem=z_send.at[way, j],
            recv_sem=z_recv.at[way, j],
            device_id=((up_d, down_d)[way], t),
            device_id_type=MESH,
        )

    def e_copy(k):
        up = d == depths - 2
        j = taken(up, k)
        return pltpu.make_async_remote_copy(
            src_ref=field.at[jnp.where(up, slices - 2, 1), :, columns(j)],
            dst_ref=f_ref.at[j + 1, jnp.where(up, Z0 - 2, Z0 + slices + 1), pl.ds(TOP, rows), :],
            send_sem=e_send.at[k],
            recv_sem=e_recv.at[k],
            device_id=(jnp.where(up, up_d, down_d), t),
            device_id_type=MESH,
        )

    def e_wait(k):
        low = d == 0
        j = taken(d > 0, k)
        pltpu.make_async_remote_copy(
            src_ref=field.at[0, :, columns(j)],
            dst_ref=f_ref.at[j + 1, jnp.where(low, Z0 + slices + 1, Z0 - 2), pl.ds(TOP, rows), :],
            send_sem=e_send.at[k],
            recv_sem=e_recv.at[k],
            device_id=(jnp.where(low, up_d, down_d), t),
            device_id_type=MESH,
        ).wait_recv()

    def x_copy(way, j):
        src, dst = ((rows - 1, TOP - 1), (0, TOP + rows))[way]
        return pltpu.make_async_remote_copy(
            src_ref=field.at[:, pl.ds(src, 1), columns(j)],
            dst_ref=f_ref.at[j + 1, pl.ds(Z0, slices), pl.ds(dst, 1), :],
            send_sem=x_send.at[way, j],
            recv_sem=x_recv.at[way, j],
            device_id=(d, (next_t, prev_t)[way]),
            device_id_type=MESH,
        )

    extra_z = jnp.where(d == 0, Z0 + slices, Z0 - 1)

    def y_copy(way, k):
        src, dst = ((TOP + rows - 1, TOP - 1), (TOP, TOP + rows))[way]
        j = taken(d > 0, k)
        return pltpu.make_async_remote_copy(
            src_ref=f_ref.at[j + 1, extra_z, pl.ds(src, 1), :],
            dst_ref=f_ref.at[j + 1, extra_z, pl.ds(dst, 1), :],
            send_sem=y_send.at[way, k],
            recv_sem=y_recv.at[way, k],
            device_id=(d, (next_t, prev_t)[way]),
            device_id_type=MESH,
        )

    def fixed_block(me, s):
        if s < per:
            off, k = 2, s
        elif s < sent:
            off, k = (1, depths - 1)[s % 2], (s - per) // 2
        else:
            off, k = 0, s - sent
        owner = me + off
        return jnp.where(owner >= depths, owner - depths, owner) * per + k

    def start_depth(s):
        j = fixed_block(up_d, s)

        @pl.when(sends_up(d, j))
        def _():
            z_copy(0, j).start()

        i = fixed_block(down_d, s)

        @pl.when(sends_down(d, i))
        def _():
            z_copy(1, i).start()

    def start_rows(s):
        j = fixed_block(d, s)

        @pl.when(has_next)
        def _():
            x_copy(0, j).start()

        @pl.when(has_prev)
        def _():
            x_copy(1, j).start()

    for s in range(blocks):
        start_depth(s)
        if s >= 2:
            start_rows(s - 2)
    for s in range(blocks - 2, blocks):
        start_rows(s)

    @pl.when(jnp.logical_not(outer))
    def _():
        for k in range(per + 1):
            e_copy(k).start()

    zeros = jnp.zeros((SUB, LANES), jnp.float32)
    for edge in (0, blocks + 1):

        def clear(i, _):
            for u in range(6):
                for row in range(0, rows, SUB):
                    f_ref[edge, 6 * i + u, pl.ds(TOP + row, SUB), :] = zeros
            return 0

        lax.fori_loop(0, (slices + 2 * Z0) // 6, clear, 0)
    for present, z, j0, j1 in (
        (d == 0, Z0 - 1, 0, blocks),
        (d == 1, Z0 - 1, 0, per),
        (d == 1, Z0 - 1, 2 * per - 1, 2 * per),
        (d == depths - 2, Z0 + slices, sent - 1, blocks),
        (d == depths - 1, Z0 + slices, 0, blocks),
    ):

        @pl.when(present)
        def _():
            for j in range(j0, j1):
                for row in range(0, rows, SUB):
                    f_ref[j + 1, z, pl.ds(TOP + row, SUB), :] = zeros

    for present, row in ((has_prev, TOP - SUB), (has_next, TOP + rows)):

        @pl.when(jnp.logical_not(present))
        def _():
            def clear(i, _):
                for j in range(4):
                    for z in range(slices + 2 * Z0):
                        f_ref[4 * i + j + 1, z, pl.ds(row, SUB), :] = zeros
                return 0

            lax.fori_loop(0, blocks // 4, clear, 0)

    for copy in params:
        copy.wait()
    for j in range(blocks):
        load(j).wait()
    shading = Shading(absorb, color, light)

    def relays_up(me, k, part):
        through = jnp.logical_or(k < SPLIT, jnp.logical_and(k == SPLIT, part == 0))
        inner = jnp.where(me == 1, through, jnp.logical_not(through))
        return jnp.logical_or(me == 0, jnp.logical_and(me < depths - 1, inner))

    def merges(way, k, part):
        from_below = jnp.logical_and(d > 0, relays_up(d - 1, k, part))
        from_above = jnp.logical_and(d < depths - 1, jnp.logical_not(relays_up(d + 1, k, part)))
        return jnp.logical_or(
            jnp.logical_and(way == 1, from_below), jnp.logical_and(way == 2, from_above)
        )

    def merges_any(way, k):
        return jnp.logical_or(merges(way, k, 0), merges(way, k, 1))

    def place(me, way, k):
        inner = jnp.where(way == 1, 0, jnp.where(way == 2, 2, 1))
        low = jnp.where(way == 1, 2, jnp.where(way == 2, 1, 0))
        high = jnp.where(way == 1, 1, jnp.where(way == 2, 0, 2))
        return sent + jnp.where(me == 0, low, jnp.where(me == depths - 1, high, inner)) * per + k

    parts = ((0, CUT), (CUT, rows - CUT))

    def relay_copy(up, s, k, part):
        way = jnp.where(up, 0, 1)
        at = pl.ds(*parts[part])
        return pltpu.make_async_remote_copy(
            src_ref=image.at[s, :, at, :],
            dst_ref=relay.at[way, k, :, at, :],
            send_sem=i_send.at[part, s],
            recv_sem=r_recv.at[way, k, part],
            device_id=(jnp.where(up, up_d, down_d), t),
            device_id_type=MESH,
        )

    def image_copy(way, s, k):
        up = way == 1
        owner = jnp.where(up, up_d, down_d)
        return pltpu.make_async_remote_copy(
            src_ref=image.at[s],
            dst_ref=image.at[place(owner, way, k)],
            send_sem=i_send.at[0, s],
            recv_sem=i_recv.at[way - 1, k],
            device_id=(owner, t),
            device_id_type=MESH,
        )

    def merge(way, s, k, part):
        relay_copy(way == 1, s, k, part).wait_recv()
        front = way == 1
        top, count = parts[part]
        for row in range(top, top + count, SUB):
            at = pl.ds(row, SUB)
            mine, other = image[s, 3, at, :], relay[way - 1, k, 3, at, :]
            one = jnp.ones_like(mine)
            a, b = jnp.where(front, other, one), jnp.where(front, one, mine)
            for c in range(3):
                image[s, c, at, :] = a * image[s, c, at, :] + b * relay[way - 1, k, c, at, :]
            image[s, 3, at, :] = mine * other

    def step(s, _):
        way, owner, k = order(d, s)
        j = owner * per + k
        own = way == 3
        shift = shifted(d, j)
        handed = jnp.logical_and(outer, shift)
        waited = jnp.logical_and(outer, own)

        @pl.when(jnp.logical_and(d > 0, jnp.logical_and(sends_up(d - 1, j), jnp.logical_not(waited))))
        def _():
            z_copy(0, j).wait_recv()

        @pl.when(jnp.logical_and(d < depths - 1, jnp.logical_and(sends_down(d + 1, j), jnp.logical_not(waited))))
        def _():
            z_copy(1, j).wait_recv()

        @pl.when(has_prev)
        def _():
            x_copy(0, j).wait_recv()

        @pl.when(has_next)
        def _():
            x_copy(1, j).wait_recv()

        @pl.when(jnp.logical_and(outer, s == sent))
        def _():
            for i in range(per):

                @pl.when(d == 0)
                def _():
                    z_copy(1, d * per + i).wait_recv()

                @pl.when(d > 0)
                def _():
                    z_copy(0, d * per + i).wait_recv()

            for i in range(per + 1):

                @pl.when(has_next)
                def _():
                    y_copy(0, i).start()

                @pl.when(has_prev)
                def _():
                    y_copy(1, i).start()

        keep_first = jnp.where(jnp.logical_and(d == 1, shift), 0.0, 1.0)
        keep_last = jnp.where(jnp.logical_and(d == depths - 2, shift), 0.0, 1.0)
        slot = jnp.where(own, place(d, 3, k), s)
        march(f_ref, j, image.at[slot], shading, keep_first, keep_last, slices, rows)

        @pl.when(way == 0)
        def _():
            for part in range(2):
                relay_copy(relays_up(d, k, part), s, k, part).start()

        near = jnp.logical_or(way == 1, way == 2)

        @pl.when(jnp.logical_and(near, jnp.logical_not(jnp.logical_or(handed, merges_any(way, k)))))
        def _():
            image_copy(way, s, k).start()

        late = jnp.maximum(s - LAG, 0)
        late_way, _, late_k = order(d, late)
        due = jnp.logical_and(s - LAG >= per, s - LAG < sent)

        for part in range(2):

            @pl.when(jnp.logical_and(due, merges(late_way, late_k, part)))
            def _():
                merge(late_way, late, late_k, part)

        @pl.when(jnp.logical_and(due, merges_any(late_way, late_k)))
        def _():
            image_copy(late_way, late, late_k).start()

        return 0

    lax.fori_loop(0, blocks, step, 0)

    @pl.when(outer)
    def _():
        def complete(n, _):
            i = jnp.where(d > 0, n, lax.rem(n + per, per + 1))
            j = taken(d > 0, i)
            e_wait(i)

            @pl.when(has_prev)
            def _():
                y_copy(0, i).wait_recv()

            @pl.when(has_next)
            def _():
                y_copy(1, i).wait_recv()

            away = n == 0
            s = jnp.where(d > 0, sent - 1, sent - 2)
            slot = jnp.where(away, s, place(d, 3, n - 1))
            march_one(f_ref, j, extra_z, image.at[slot], shading, d > 0, rows)

            @pl.when(away)
            def _():
                image_copy(jnp.where(d > 0, 2, 1), s, per - 1).start()

            return 0

        lax.fori_loop(0, per + 1, complete, 0)

    def drain(j, _):
        @pl.when(sends_up(d, j))
        def _():
            z_copy(0, j).wait_send()

        @pl.when(sends_down(d, j))
        def _():
            z_copy(1, j).wait_send()

        @pl.when(has_next)
        def _():
            x_copy(0, j).wait_send()

        @pl.when(has_prev)
        def _():
            x_copy(1, j).wait_send()

        return 0

    lax.fori_loop(0, blocks, drain, 0)

    for k in range(per + 1):

        @pl.when(jnp.logical_not(outer))
        def _():
            e_copy(k).wait_send()

        @pl.when(jnp.logical_and(outer, has_next))
        def _():
            y_copy(0, k).wait_send()

        @pl.when(jnp.logical_and(outer, has_prev))
        def _():
            y_copy(1, k).wait_send()

    def compose(k, _):
        for way in (1, 2):
            pltpu.make_async_remote_copy(
                src_ref=image.at[0],
                dst_ref=image.at[place(d, way, k)],
                send_sem=i_send.at[0, 0],
                recv_sem=i_recv.at[way - 1, k],
                device_id=(up_d, t),
                device_id_type=MESH,
            ).wait_recv()
        for top in range(0, rows, SUB):
            at = pl.ds(top, SUB)
            seen = image[sent + k, 3, at, :]
            total = [image[sent + k, c, at, :] for c in range(3)]
            for q in (sent + per + k, sent + 2 * per + k):
                total = [total[c] + seen * image[q, c, at, :] for c in range(3)]
                seen = seen * image[q, 3, at, :]
            for c in range(3):
                out[c, at, columns(k)] = total[c]
            out[3, at, columns(k)] = 1.0 - seen
        return 0

    lax.fori_loop(0, per, compose, 0)

    for s in range(sent):
        if s < per:
            for part in range(2):
                relay_copy(d == 0, s, 0, part).wait_send()
        else:
            image_copy(jnp.where(d >= 0, 1, 2), s, 0).wait_send()


def on_device(depths, tiles, field, absorb, color, light):
    slices, rows, columns = field.shape
    blocks = columns // LANES
    per = blocks // depths
    sent = (depths - 1) * per
    dma = pltpu.SemaphoreType.DMA
    return pl.pallas_call(
        functools.partial(kernel, depths, tiles, slices, rows, blocks),
        out_shape=pltpu.VMEM((4, rows, columns // depths), jnp.float32),
        in_specs=[pl.BlockSpec(memory_space=pl.ANY)] * 4,
        out_specs=pl.BlockSpec(memory_space=pltpu.VMEM),
        scratch_shapes=[
            pltpu.VMEM((blocks + 2, slices + 2 * Z0, rows + 2 * TOP, LANES), jnp.float32),
            pltpu.VMEM((sent + 3 * per, 4, rows, LANES), jnp.float32),
            pltpu.VMEM((2, per, 4, rows, LANES), jnp.float32),
            pltpu.SMEM((2,), jnp.float32),
            pltpu.SMEM((3, 4), jnp.float32),
            pltpu.SMEM((3,), jnp.float32),
            dma((3,)),
            dma((blocks,)),
            dma((2, blocks)),
            dma((2, blocks)),
            dma((per + 1,)),
            dma((per + 1,)),
            dma((2, blocks)),
            dma((2, blocks)),
            dma((2, per + 1)),
            dma((2, per + 1)),
            dma((2, sent)),
            dma((2, per, 2)),
            dma((2, per)),
        ],
        compiler_params=pltpu.CompilerParams(
            collective_id=0, has_side_effects=True, vmem_limit_bytes=55 << 20
        ),
    )(field, absorb, color, light)


def solution(mesh):
    depths, tiles = mesh.shape["depth"], mesh.shape["tile"]
    return jax.shard_map(
        functools.partial(on_device, depths, tiles),
        mesh=mesh,
        in_specs=(P("depth", "tile", None), P(), P(), P()),
        out_specs=P(None, "tile", "depth"),
        check_vma=False,
    )
```

```python
import functools
import math

import jax
import jax.numpy as jnp
from jax import lax
from jax.experimental import pallas as pl
from jax.experimental.pallas import tpu as pltpu
from jax.sharding import PartitionSpec as P

MESH = pl.DeviceIdType.MESH
LANES = 128
SUB = 8
TOP = 8
Z0 = 2
GROUP = 2
UNROLL = 16
LAG = 3
SPLIT = 2
CUT = 40


class Shading:
    def __init__(self, absorb, color, light):
        self.base = -absorb[0] * math.log2(math.e)
        self.slope = -absorb[1] * math.log2(math.e)
        self.light = light[0], light[1], light[2]
        self.color = color

    def facing_and_norm(self, dz, dx, dy):
        lz, lx, ly = self.light
        facing = jnp.abs(lz * dz + lx * dx + ly * dy)
        return facing * lax.rsqrt((dz * dz + 4.0) + (dx * dx + dy * dy))

    def channel(self, c, m0, m1, m2, m3):
        color = self.color
        return (color[c, 0] * m0 + color[c, 1] * m1) + (color[c, 2] * m2 + color[c, 3] * m3)


def sideways(f_ref, j, z, row):
    lane = lax.broadcasted_iota(jnp.int32, (SUB, LANES), 1)
    f = f_ref[j + 1, z, pl.ds(row, SUB), :]
    left = jnp.where(lane == LANES - 1, f_ref[j, z, pl.ds(row, SUB), :], f)
    right = jnp.where(lane == 0, f_ref[j + 2, z, pl.ds(row, SUB), :], f)
    return pltpu.roll(right, LANES - 1, 1) - pltpu.roll(left, 1, 1)


def rowwise(f_ref, j, z, row):
    return f_ref[j + 1, z, pl.ds(row + 1, SUB), :] - f_ref[j + 1, z, pl.ds(row - 1, SUB), :]


def march(f_ref, j, dst, shading, keep_first, keep_last, slices, rows):
    first = shading.base * keep_first, shading.slope * keep_first
    last = shading.base * keep_last, shading.slope * keep_last

    for top in range(0, rows, GROUP * SUB):
        starts = [TOP + top + SUB * r for r in range(GROUP)]

        def across(s0):
            return [sideways(f_ref, j, Z0 + s0 + u, row) for row in starts for u in range(UNROLL)]

        one = jnp.ones((SUB, LANES), jnp.float32)
        zero = jnp.zeros((SUB, LANES), jnp.float32)
        state = [[one, zero, zero, zero, zero] for _ in range(GROUP)]
        ahead = across(0)
        for s0 in range(0, slices, UNROLL):
            now = ahead
            if s0 + UNROLL < slices:
                ahead = across(s0 + UNROLL)
            for r, row in enumerate(starts):
                here = [f_ref[j + 1, Z0 + s0 + u - 1, pl.ds(row, SUB), :] for u in range(UNROLL + 2)]
                for u in range(UNROLL):
                    below, f, above = here[u], here[u + 1], here[u + 2]
                    dx = rowwise(f_ref, j, Z0 + s0 + u, row)
                    shade = shading.facing_and_norm(above - below, dx, now[r * UNROLL + u])
                    base, slope = shading.base, shading.slope
                    if s0 + u == 0:
                        base, slope = first
                    if s0 + u == slices - 1:
                        base, slope = last
                    f2 = f * f
                    t, m0, m1, m2, m3 = state[r]
                    behind = t * jnp.exp2(base + slope * f2)
                    w0 = (t - behind) * shade
                    w1 = w0 * f
                    state[r] = [behind, m0 + w0, m1 + w1, m2 + w0 * f2, m3 + w1 * f2]
        for r in range(GROUP):
            t, *moments = state[r]
            at = pl.ds(top + SUB * r, SUB)
            for c in range(3):
                dst[c, at, :] = shading.channel(c, *moments)
            dst[3, at, :] = t


def march_one(f_ref, j, z, dst, shading, in_front, rows):
    def tile(top):
        row = top + TOP
        f = f_ref[j + 1, z, pl.ds(row, SUB), :]
        dz = f_ref[j + 1, z + 1, pl.ds(row, SUB), :] - f_ref[j + 1, z - 1, pl.ds(row, SUB), :]
        shade = shading.facing_and_norm(dz, rowwise(f_ref, j, z, row), sideways(f_ref, j, z, row))
        f2 = f * f
        passed = jnp.exp2(shading.base + shading.slope * f2)
        w0 = (1.0 - passed) * shade
        w1 = w0 * f
        at = pl.ds(top, SUB)
        seen = dst[3, at, :]
        one = jnp.ones_like(seen)
        old = jnp.where(in_front, passed, one)
        new = jnp.where(in_front, one, seen)
        for c in range(3):
            dst[c, at, :] = old * dst[c, at, :] + new * shading.channel(c, w0, w1, w0 * f2, w1 * f2)
        dst[3, at, :] = seen * passed

    for top in range(0, rows, SUB):
        tile(top)


def kernel(
    depths, tiles, slices, rows, blocks,
    field, absorb_in, color_in, light_in, out,
    f_ref, image, relay, absorb, color, light,
    param_sem, load_sem, z_send, z_recv, e_send, e_recv, x_send, x_recv, y_send, y_recv,
    i_send, r_recv, i_recv,
):
    d, t = lax.axis_index("depth"), lax.axis_index("tile")
    per = blocks // depths
    sent = (depths - 1) * per
    up_d, down_d = lax.rem(d + 1, depths), lax.rem(d + depths - 1, depths)
    next_t, prev_t = lax.rem(t + 1, tiles), lax.rem(t + tiles - 1, tiles)
    has_prev, has_next = t > 0, t < tiles - 1
    outer = jnp.logical_or(d == 0, d == depths - 1)

    params = [
        pltpu.make_async_copy(src, dst, param_sem.at[i])
        for i, (src, dst) in enumerate(((absorb_in, absorb), (color_in, color), (light_in, light)))
    ]

    def columns(j):
        return pl.ds(pl.multiple_of(j * LANES, LANES), LANES)

    def load(j):
        return pltpu.make_async_copy(
            field.at[:, :, columns(j)],
            f_ref.at[j + 1, pl.ds(Z0, slices), pl.ds(TOP, rows), :],
            load_sem.at[j],
        )

    barrier = pltpu.get_barrier_semaphore()
    for peer in (up_d, down_d):
        pl.semaphore_signal(barrier, inc=1, device_id=(peer, t), device_id_type=MESH)
    for present, peer in ((has_next, next_t), (has_prev, prev_t)):

        @pl.when(present)
        def _():
            pl.semaphore_signal(barrier, inc=1, device_id=(d, peer), device_id_type=MESH)

    for copy in params:
        copy.start()
    for j in range(blocks):
        load(j).start()

    beside = has_prev.astype(jnp.int32) + has_next.astype(jnp.int32)
    pl.semaphore_wait(barrier, 2 + beside)

    def order(me, s):
        far, own = s < per, s >= sent
        way = jnp.where(far, 0, jnp.where(own, 3, 1 + lax.rem(s, 2)))
        k = jnp.where(far, s, jnp.where(own, s - sent, (s - per) // 2))
        off = jnp.where(way == 0, 2, jnp.where(way == 1, 1, jnp.where(way == 2, depths - 1, 0)))
        return way, lax.rem(me + off, depths), k

    def block(me, s):
        _, owner, k = order(me, s)
        return owner * per + k

    def shifted(me, j):
        low = jnp.logical_or(j < per, j == 2 * per - 1)
        return jnp.where(me < depths // 2, low, j >= sent - 1)

    def taken(high, i):
        return jnp.where(high, sent - 1 + i, jnp.where(i < per, i, 2 * per - 1))

    def sends_up(me, j):
        return jnp.logical_and(me < depths - 1, jnp.logical_not(jnp.logical_and(me == 0, shifted(me, j))))

    def sends_down(me, j):
        return jnp.logical_and(me > 0, jnp.logical_not(jnp.logical_and(me == depths - 1, shifted(me, j))))

    def z_copy(way, j):
        src, dst = ((slices - 1, Z0 - 1), (0, Z0 + slices))[way]
        return pltpu.make_async_remote_copy(
            src_ref=field.at[src, :, columns(j)],
            dst_ref=f_ref.at[j + 1, dst, pl.ds(TOP, rows), :],
            send_sem=z_send.at[way, j],
            recv_sem=z_recv.at[way, j],
            device_id=((up_d, down_d)[way], t),
            device_id_type=MESH,
        )

    def e_copy(k):
        up = d == depths - 2
        j = taken(up, k)
        return pltpu.make_async_remote_copy(
            src_ref=field.at[jnp.where(up, slices - 2, 1), :, columns(j)],
            dst_ref=f_ref.at[j + 1, jnp.where(up, Z0 - 2, Z0 + slices + 1), pl.ds(TOP, rows), :],
            send_sem=e_send.at[k],
            recv_sem=e_recv.at[k],
            device_id=(jnp.where(up, up_d, down_d), t),
            device_id_type=MESH,
        )

    def e_wait(k):
        low = d == 0
        j = taken(d > 0, k)
        pltpu.make_async_remote_copy(
            src_ref=field.at[0, :, columns(j)],
            dst_ref=f_ref.at[j + 1, jnp.where(low, Z0 + slices + 1, Z0 - 2), pl.ds(TOP, rows), :],
            send_sem=e_send.at[k],
            recv_sem=e_recv.at[k],
            device_id=(jnp.where(low, up_d, down_d), t),
            device_id_type=MESH,
        ).wait_recv()

    def x_copy(way, j):
        src, dst = ((rows - 1, TOP - 1), (0, TOP + rows))[way]
        return pltpu.make_async_remote_copy(
            src_ref=field.at[:, pl.ds(src, 1), columns(j)],
            dst_ref=f_ref.at[j + 1, pl.ds(Z0, slices), pl.ds(dst, 1), :],
            send_sem=x_send.at[way, j],
            recv_sem=x_recv.at[way, j],
            device_id=(d, (next_t, prev_t)[way]),
            device_id_type=MESH,
        )

    extra_z = jnp.where(d == 0, Z0 + slices, Z0 - 1)

    def y_copy(way, k):
        src, dst = ((TOP + rows - 1, TOP - 1), (TOP, TOP + rows))[way]
        j = taken(d > 0, k)
        return pltpu.make_async_remote_copy(
            src_ref=f_ref.at[j + 1, extra_z, pl.ds(src, 1), :],
            dst_ref=f_ref.at[j + 1, extra_z, pl.ds(dst, 1), :],
            send_sem=y_send.at[way, k],
            recv_sem=y_recv.at[way, k],
            device_id=(d, (next_t, prev_t)[way]),
            device_id_type=MESH,
        )

    def fixed_block(me, s):
        if s < per:
            off, k = 2, s
        elif s < sent:
            off, k = (1, depths - 1)[s % 2], (s - per) // 2
        else:
            off, k = 0, s - sent
        owner = me + off
        return jnp.where(owner >= depths, owner - depths, owner) * per + k

    def start_depth(s):
        j = fixed_block(up_d, s)

        @pl.when(sends_up(d, j))
        def _():
            z_copy(0, j).start()

        i = fixed_block(down_d, s)

        @pl.when(sends_down(d, i))
        def _():
            z_copy(1, i).start()

    def start_rows(s):
        j = fixed_block(d, s)

        @pl.when(has_next)
        def _():
            x_copy(0, j).start()

        @pl.when(has_prev)
        def _():
            x_copy(1, j).start()

    for s in range(blocks):
        start_depth(s)
        if s >= 2:
            start_rows(s - 2)
    for s in range(blocks - 2, blocks):
        start_rows(s)

    @pl.when(jnp.logical_not(outer))
    def _():
        for k in range(per + 1):
            e_copy(k).start()

    zeros = jnp.zeros((SUB, LANES), jnp.float32)
    for edge in (0, blocks + 1):

        def clear(i, _):
            for u in range(6):
                for row in range(0, rows, SUB):
                    f_ref[edge, 6 * i + u, pl.ds(TOP + row, SUB), :] = zeros
            return 0

        lax.fori_loop(0, (slices + 2 * Z0) // 6, clear, 0)
    for present, z, j0, j1 in (
        (d == 0, Z0 - 1, 0, blocks),
        (d == 1, Z0 - 1, 0, per),
        (d == 1, Z0 - 1, 2 * per - 1, 2 * per),
        (d == depths - 2, Z0 + slices, sent - 1, blocks),
        (d == depths - 1, Z0 + slices, 0, blocks),
    ):

        @pl.when(present)
        def _():
            for j in range(j0, j1):
                for row in range(0, rows, SUB):
                    f_ref[j + 1, z, pl.ds(TOP + row, SUB), :] = zeros

    for present, row in ((has_prev, TOP - SUB), (has_next, TOP + rows)):

        @pl.when(jnp.logical_not(present))
        def _():
            def clear(i, _):
                for j in range(4):
                    for z in range(slices + 2 * Z0):
                        f_ref[4 * i + j + 1, z, pl.ds(row, SUB), :] = zeros
                return 0

            lax.fori_loop(0, blocks // 4, clear, 0)

    for copy in params:
        copy.wait()
    for j in range(blocks):
        load(j).wait()
    shading = Shading(absorb, color, light)

    def relays_up(me, k, part):
        through = jnp.logical_or(k < SPLIT, jnp.logical_and(k == SPLIT, part == 0))
        inner = jnp.where(me == 1, through, jnp.logical_not(through))
        return jnp.logical_or(me == 0, jnp.logical_and(me < depths - 1, inner))

    def merges(way, k, part):
        from_below = jnp.logical_and(d > 0, relays_up(d - 1, k, part))
        from_above = jnp.logical_and(d < depths - 1, jnp.logical_not(relays_up(d + 1, k, part)))
        return jnp.logical_or(
            jnp.logical_and(way == 1, from_below), jnp.logical_and(way == 2, from_above)
        )

    def merges_any(way, k):
        return jnp.logical_or(merges(way, k, 0), merges(way, k, 1))

    def place(me, way, k):
        inner = jnp.where(way == 1, 0, jnp.where(way == 2, 2, 1))
        low = jnp.where(way == 1, 2, jnp.where(way == 2, 1, 0))
        high = jnp.where(way == 1, 1, jnp.where(way == 2, 0, 2))
        return sent + jnp.where(me == 0, low, jnp.where(me == depths - 1, high, inner)) * per + k

    parts = ((0, CUT), (CUT, rows - CUT))

    def relay_copy(up, s, k, part):
        way = jnp.where(up, 0, 1)
        at = pl.ds(*parts[part])
        return pltpu.make_async_remote_copy(
            src_ref=image.at[s, :, at, :],
            dst_ref=relay.at[way, k, :, at, :],
            send_sem=i_send.at[part, s],
            recv_sem=r_recv.at[way, k, part],
            device_id=(jnp.where(up, up_d, down_d), t),
            device_id_type=MESH,
        )

    def image_copy(way, s, k):
        up = way == 1
        owner = jnp.where(up, up_d, down_d)
        return pltpu.make_async_remote_copy(
            src_ref=image.at[s],
            dst_ref=image.at[place(owner, way, k)],
            send_sem=i_send.at[0, s],
            recv_sem=i_recv.at[way - 1, k],
            device_id=(owner, t),
            device_id_type=MESH,
        )

    def merge(way, s, k, part):
        relay_copy(way == 1, s, k, part).wait_recv()
        front = way == 1
        top, count = parts[part]
        for row in range(top, top + count, SUB):
            at = pl.ds(row, SUB)
            mine, other = image[s, 3, at, :], relay[way - 1, k, 3, at, :]
            one = jnp.ones_like(mine)
            a, b = jnp.where(front, other, one), jnp.where(front, one, mine)
            for c in range(3):
                image[s, c, at, :] = a * image[s, c, at, :] + b * relay[way - 1, k, c, at, :]
            image[s, 3, at, :] = mine * other

    def step(s, _):
        way, owner, k = order(d, s)
        j = owner * per + k
        own = way == 3
        shift = shifted(d, j)
        handed = jnp.logical_and(outer, shift)
        waited = jnp.logical_and(outer, own)

        @pl.when(jnp.logical_and(d > 0, jnp.logical_and(sends_up(d - 1, j), jnp.logical_not(waited))))
        def _():
            z_copy(0, j).wait_recv()

        @pl.when(jnp.logical_and(d < depths - 1, jnp.logical_and(sends_down(d + 1, j), jnp.logical_not(waited))))
        def _():
            z_copy(1, j).wait_recv()

        @pl.when(has_prev)
        def _():
            x_copy(0, j).wait_recv()

        @pl.when(has_next)
        def _():
            x_copy(1, j).wait_recv()

        @pl.when(jnp.logical_and(outer, s == sent))
        def _():
            for i in range(per):

                @pl.when(d == 0)
                def _():
                    z_copy(1, d * per + i).wait_recv()

                @pl.when(d > 0)
                def _():
                    z_copy(0, d * per + i).wait_recv()

            for i in range(per + 1):

                @pl.when(has_next)
                def _():
                    y_copy(0, i).start()

                @pl.when(has_prev)
                def _():
                    y_copy(1, i).start()

        keep_first = jnp.where(jnp.logical_and(d == 1, shift), 0.0, 1.0)
        keep_last = jnp.where(jnp.logical_and(d == depths - 2, shift), 0.0, 1.0)
        slot = jnp.where(own, place(d, 3, k), s)
        march(f_ref, j, image.at[slot], shading, keep_first, keep_last, slices, rows)

        @pl.when(way == 0)
        def _():
            for part in range(2):
                relay_copy(relays_up(d, k, part), s, k, part).start()

        near = jnp.logical_or(way == 1, way == 2)

        @pl.when(jnp.logical_and(near, jnp.logical_not(jnp.logical_or(handed, merges_any(way, k)))))
        def _():
            image_copy(way, s, k).start()

        late = jnp.maximum(s - LAG, 0)
        late_way, _, late_k = order(d, late)
        due = jnp.logical_and(s - LAG >= per, s - LAG < sent)

        for part in range(2):

            @pl.when(jnp.logical_and(due, merges(late_way, late_k, part)))
            def _():
                merge(late_way, late, late_k, part)

        @pl.when(jnp.logical_and(due, merges_any(late_way, late_k)))
        def _():
            image_copy(late_way, late, late_k).start()

        return 0

    lax.fori_loop(0, blocks, step, 0)

    @pl.when(outer)
    def _():
        def complete(n, _):
            i = jnp.where(d > 0, n, lax.rem(n + per, per + 1))
            j = taken(d > 0, i)
            e_wait(i)

            @pl.when(has_prev)
            def _():
                y_copy(0, i).wait_recv()

            @pl.when(has_next)
            def _():
                y_copy(1, i).wait_recv()

            away = n == 0
            s = jnp.where(d > 0, sent - 1, sent - 2)
            slot = jnp.where(away, s, place(d, 3, n - 1))
            march_one(f_ref, j, extra_z, image.at[slot], shading, d > 0, rows)

            @pl.when(away)
            def _():
                image_copy(jnp.where(d > 0, 2, 1), s, per - 1).start()

            return 0

        lax.fori_loop(0, per + 1, complete, 0)

    def drain(j, _):
        @pl.when(sends_up(d, j))
        def _():
            z_copy(0, j).wait_send()

        @pl.when(sends_down(d, j))
        def _():
            z_copy(1, j).wait_send()

        @pl.when(has_next)
        def _():
            x_copy(0, j).wait_send()

        @pl.when(has_prev)
        def _():
            x_copy(1, j).wait_send()

        return 0

    lax.fori_loop(0, blocks, drain, 0)

    for k in range(per + 1):

        @pl.when(jnp.logical_not(outer))
        def _():
            e_copy(k).wait_send()

        @pl.when(jnp.logical_and(outer, has_next))
        def _():
            y_copy(0, k).wait_send()

        @pl.when(jnp.logical_and(outer, has_prev))
        def _():
            y_copy(1, k).wait_send()

    def compose(k, _):
        for way in (1, 2):
            pltpu.make_async_remote_copy(
                src_ref=image.at[0],
                dst_ref=image.at[place(d, way, k)],
                send_sem=i_send.at[0, 0],
                recv_sem=i_recv.at[way - 1, k],
                device_id=(up_d, t),
                device_id_type=MESH,
            ).wait_recv()
        for top in range(0, rows, SUB):
            at = pl.ds(top, SUB)
            seen = image[sent + k, 3, at, :]
            total = [image[sent + k, c, at, :] for c in range(3)]
            for q in (sent + per + k, sent + 2 * per + k):
                total = [total[c] + seen * image[q, c, at, :] for c in range(3)]
                seen = seen * image[q, 3, at, :]
            for c in range(3):
                out[c, at, columns(k)] = total[c]
            out[3, at, columns(k)] = 1.0 - seen
        return 0

    lax.fori_loop(0, per, compose, 0)

    for s in range(sent):
        if s < per:
            for part in range(2):
                relay_copy(d == 0, s, 0, part).wait_send()
        else:
            image_copy(jnp.where(d >= 0, 1, 2), s, 0).wait_send()


def on_device(depths, tiles, field, absorb, color, light):
    slices, rows, columns = field.shape
    blocks = columns // LANES
    per = blocks // depths
    sent = (depths - 1) * per
    dma = pltpu.SemaphoreType.DMA
    return pl.pallas_call(
        functools.partial(kernel, depths, tiles, slices, rows, blocks),
        out_shape=pltpu.VMEM((4, rows, columns // depths), jnp.float32),
        in_specs=[pl.BlockSpec(memory_space=pl.ANY)] * 4,
        out_specs=pl.BlockSpec(memory_space=pltpu.VMEM),
        scratch_shapes=[
            pltpu.VMEM((blocks + 2, slices + 2 * Z0, rows + 2 * TOP, LANES), jnp.float32),
            pltpu.VMEM((sent + 3 * per, 4, rows, LANES), jnp.float32),
            pltpu.VMEM((2, per, 4, rows, LANES), jnp.float32),
            pltpu.SMEM((2,), jnp.float32),
            pltpu.SMEM((3, 4), jnp.float32),
            pltpu.SMEM((3,), jnp.float32),
            dma((3,)),
            dma((blocks,)),
            dma((2, blocks)),
            dma((2, blocks)),
            dma((per + 1,)),
            dma((per + 1,)),
            dma((2, blocks)),
            dma((2, blocks)),
            dma((2, per + 1)),
            dma((2, per + 1)),
            dma((2, sent)),
            dma((2, per, 2)),
            dma((2, per)),
        ],
        compiler_params=pltpu.CompilerParams(
            collective_id=0, has_side_effects=True, vmem_limit_bytes=55 << 20
        ),
    )(field, absorb, color, light)


def solution(mesh):
    depths, tiles = mesh.shape["depth"], mesh.shape["tile"]
    return jax.shard_map(
        functools.partial(on_device, depths, tiles),
        mesh=mesh,
        in_specs=(P("depth", "tile", None), P(), P(), P()),
        out_specs=P(None, "tile", "depth"),
        check_vma=False,
    )
```

```python
import functools
import math

import jax
import jax.numpy as jnp
from jax import lax
from jax.experimental import pallas as pl
from jax.experimental.pallas import tpu as pltpu
from jax.sharding import PartitionSpec as P

MESH = pl.DeviceIdType.MESH
LANES = 128
SUB = 8
TOP = 8
Z0 = 2
GROUP = 2
UNROLL = 16
LAG = 2
SPLIT = 2
CUT = 40


class Shading:
    def __init__(self, absorb, color, light):
        self.base = -absorb[0] * math.log2(math.e)
        self.slope = -absorb[1] * math.log2(math.e)
        self.light = light[0], light[1], light[2]
        self.color = color

    def facing_and_norm(self, dz, dx, dy):
        lz, lx, ly = self.light
        facing = jnp.abs(lz * dz + lx * dx + ly * dy)
        return facing * lax.rsqrt((dz * dz + 4.0) + (dx * dx + dy * dy))

    def channel(self, c, m0, m1, m2, m3):
        color = self.color
        return (color[c, 0] * m0 + color[c, 1] * m1) + (color[c, 2] * m2 + color[c, 3] * m3)


def sideways(f_ref, j, z, row):
    lane = lax.broadcasted_iota(jnp.int32, (SUB, LANES), 1)
    f = f_ref[j + 1, z, pl.ds(row, SUB), :]
    left = jnp.where(lane == LANES - 1, f_ref[j, z, pl.ds(row, SUB), :], f)
    right = jnp.where(lane == 0, f_ref[j + 2, z, pl.ds(row, SUB), :], f)
    return pltpu.roll(right, LANES - 1, 1) - pltpu.roll(left, 1, 1)


def rowwise(f_ref, j, z, row):
    return f_ref[j + 1, z, pl.ds(row + 1, SUB), :] - f_ref[j + 1, z, pl.ds(row - 1, SUB), :]


def march(f_ref, j, dst, shading, keep_first, keep_last, slices, rows):
    first = shading.base * keep_first, shading.slope * keep_first
    last = shading.base * keep_last, shading.slope * keep_last

    for top in range(0, rows, GROUP * SUB):
        starts = [TOP + top + SUB * r for r in range(GROUP)]

        def across(s0):
            return [sideways(f_ref, j, Z0 + s0 + u, row) for row in starts for u in range(UNROLL)]

        one = jnp.ones((SUB, LANES), jnp.float32)
        zero = jnp.zeros((SUB, LANES), jnp.float32)
        state = [[one, zero, zero, zero, zero] for _ in range(GROUP)]
        ahead = across(0)
        for s0 in range(0, slices, UNROLL):
            now = ahead
            if s0 + UNROLL < slices:
                ahead = across(s0 + UNROLL)
            for r, row in enumerate(starts):
                here = [f_ref[j + 1, Z0 + s0 + u - 1, pl.ds(row, SUB), :] for u in range(UNROLL + 2)]
                for u in range(UNROLL):
                    below, f, above = here[u], here[u + 1], here[u + 2]
                    dx = rowwise(f_ref, j, Z0 + s0 + u, row)
                    shade = shading.facing_and_norm(above - below, dx, now[r * UNROLL + u])
                    base, slope = shading.base, shading.slope
                    if s0 + u == 0:
                        base, slope = first
                    if s0 + u == slices - 1:
                        base, slope = last
                    f2 = f * f
                    t, m0, m1, m2, m3 = state[r]
                    behind = t * jnp.exp2(base + slope * f2)
                    w0 = (t - behind) * shade
                    w1 = w0 * f
                    state[r] = [behind, m0 + w0, m1 + w1, m2 + w0 * f2, m3 + w1 * f2]
        for r in range(GROUP):
            t, *moments = state[r]
            at = pl.ds(top + SUB * r, SUB)
            for c in range(3):
                dst[c, at, :] = shading.channel(c, *moments)
            dst[3, at, :] = t


def march_one(f_ref, j, z, dst, shading, in_front, rows):
    def tile(top):
        row = top + TOP
        f = f_ref[j + 1, z, pl.ds(row, SUB), :]
        dz = f_ref[j + 1, z + 1, pl.ds(row, SUB), :] - f_ref[j + 1, z - 1, pl.ds(row, SUB), :]
        shade = shading.facing_and_norm(dz, rowwise(f_ref, j, z, row), sideways(f_ref, j, z, row))
        f2 = f * f
        passed = jnp.exp2(shading.base + shading.slope * f2)
        w0 = (1.0 - passed) * shade
        w1 = w0 * f
        at = pl.ds(top, SUB)
        seen = dst[3, at, :]
        one = jnp.ones_like(seen)
        old = jnp.where(in_front, passed, one)
        new = jnp.where(in_front, one, seen)
        for c in range(3):
            dst[c, at, :] = old * dst[c, at, :] + new * shading.channel(c, w0, w1, w0 * f2, w1 * f2)
        dst[3, at, :] = seen * passed

    for top in range(0, rows, SUB):
        tile(top)


def kernel(
    depths, tiles, slices, rows, blocks,
    field, absorb_in, color_in, light_in, out,
    f_ref, image, relay, absorb, color, light,
    param_sem, load_sem, z_send, z_recv, e_send, e_recv, x_send, x_recv, y_send, y_recv,
    i_send, r_recv, i_recv,
):
    d, t = lax.axis_index("depth"), lax.axis_index("tile")
    per = blocks // depths
    sent = (depths - 1) * per
    up_d, down_d = lax.rem(d + 1, depths), lax.rem(d + depths - 1, depths)
    next_t, prev_t = lax.rem(t + 1, tiles), lax.rem(t + tiles - 1, tiles)
    has_prev, has_next = t > 0, t < tiles - 1
    outer = jnp.logical_or(d == 0, d == depths - 1)

    params = [
        pltpu.make_async_copy(src, dst, param_sem.at[i])
        for i, (src, dst) in enumerate(((absorb_in, absorb), (color_in, color), (light_in, light)))
    ]

    def columns(j):
        return pl.ds(pl.multiple_of(j * LANES, LANES), LANES)

    def load(j):
        return pltpu.make_async_copy(
            field.at[:, :, columns(j)],
            f_ref.at[j + 1, pl.ds(Z0, slices), pl.ds(TOP, rows), :],
            load_sem.at[j],
        )

    barrier = pltpu.get_barrier_semaphore()
    for peer in (up_d, down_d):
        pl.semaphore_signal(barrier, inc=1, device_id=(peer, t), device_id_type=MESH)
    for present, peer in ((has_next, next_t), (has_prev, prev_t)):

        @pl.when(present)
        def _():
            pl.semaphore_signal(barrier, inc=1, device_id=(d, peer), device_id_type=MESH)

    for copy in params:
        copy.start()
    for j in range(blocks):
        load(j).start()

    beside = has_prev.astype(jnp.int32) + has_next.astype(jnp.int32)
    pl.semaphore_wait(barrier, 2 + beside)

    def order(me, s):
        far, own = s < per, s >= sent
        way = jnp.where(far, 0, jnp.where(own, 3, 1 + lax.rem(s, 2)))
        k = jnp.where(far, s, jnp.where(own, s - sent, (s - per) // 2))
        off = jnp.where(way == 0, 2, jnp.where(way == 1, 1, jnp.where(way == 2, depths - 1, 0)))
        return way, lax.rem(me + off, depths), k

    def block(me, s):
        _, owner, k = order(me, s)
        return owner * per + k

    def shifted(me, j):
        low = jnp.logical_or(j < per, j == 2 * per - 1)
        return jnp.where(me < depths // 2, low, j >= sent - 1)

    def taken(high, i):
        return jnp.where(high, sent - 1 + i, jnp.where(i < per, i, 2 * per - 1))

    def sends_up(me, j):
        return jnp.logical_and(me < depths - 1, jnp.logical_not(jnp.logical_and(me == 0, shifted(me, j))))

    def sends_down(me, j):
        return jnp.logical_and(me > 0, jnp.logical_not(jnp.logical_and(me == depths - 1, shifted(me, j))))

    def z_copy(way, j):
        src, dst = ((slices - 1, Z0 - 1), (0, Z0 + slices))[way]
        return pltpu.make_async_remote_copy(
            src_ref=field.at[src, :, columns(j)],
            dst_ref=f_ref.at[j + 1, dst, pl.ds(TOP, rows), :],
            send_sem=z_send.at[way, j],
            recv_sem=z_recv.at[way, j],
            device_id=((up_d, down_d)[way], t),
            device_id_type=MESH,
        )

    def e_copy(k):
        up = d == depths - 2
        j = taken(up, k)
        return pltpu.make_async_remote_copy(
            src_ref=field.at[jnp.where(up, slices - 2, 1), :, columns(j)],
            dst_ref=f_ref.at[j + 1, jnp.where(up, Z0 - 2, Z0 + slices + 1), pl.ds(TOP, rows), :],
            send_sem=e_send.at[k],
            recv_sem=e_recv.at[k],
            device_id=(jnp.where(up, up_d, down_d), t),
            device_id_type=MESH,
        )

    def e_wait(k):
        low = d == 0
        j = taken(d > 0, k)
        pltpu.make_async_remote_copy(
            src_ref=field.at[0, :, columns(j)],
            dst_ref=f_ref.at[j + 1, jnp.where(low, Z0 + slices + 1, Z0 - 2), pl.ds(TOP, rows), :],
            send_sem=e_send.at[k],
            recv_sem=e_recv.at[k],
            device_id=(jnp.where(low, up_d, down_d), t),
            device_id_type=MESH,
        ).wait_recv()

    def x_copy(way, j):
        src, dst = ((rows - 1, TOP - 1), (0, TOP + rows))[way]
        return pltpu.make_async_remote_copy(
            src_ref=field.at[:, pl.ds(src, 1), columns(j)],
            dst_ref=f_ref.at[j + 1, pl.ds(Z0, slices), pl.ds(dst, 1), :],
            send_sem=x_send.at[way, j],
            recv_sem=x_recv.at[way, j],
            device_id=(d, (next_t, prev_t)[way]),
            device_id_type=MESH,
        )

    extra_z = jnp.where(d == 0, Z0 + slices, Z0 - 1)

    def y_copy(way, k):
        src, dst = ((TOP + rows - 1, TOP - 1), (TOP, TOP + rows))[way]
        j = taken(d > 0, k)
        return pltpu.make_async_remote_copy(
            src_ref=f_ref.at[j + 1, extra_z, pl.ds(src, 1), :],
            dst_ref=f_ref.at[j + 1, extra_z, pl.ds(dst, 1), :],
            send_sem=y_send.at[way, k],
            recv_sem=y_recv.at[way, k],
            device_id=(d, (next_t, prev_t)[way]),
            device_id_type=MESH,
        )

    def fixed_block(me, s):
        if s < per:
            off, k = 2, s
        elif s < sent:
            off, k = (1, depths - 1)[s % 2], (s - per) // 2
        else:
            off, k = 0, s - sent
        owner = me + off
        return jnp.where(owner >= depths, owner - depths, owner) * per + k

    def start_depth(s):
        j = fixed_block(up_d, s)

        @pl.when(sends_up(d, j))
        def _():
            z_copy(0, j).start()

        i = fixed_block(down_d, s)

        @pl.when(sends_down(d, i))
        def _():
            z_copy(1, i).start()

    def start_rows(s):
        j = fixed_block(d, s)

        @pl.when(has_next)
        def _():
            x_copy(0, j).start()

        @pl.when(has_prev)
        def _():
            x_copy(1, j).start()

    for s in range(blocks):
        start_depth(s)
        if s >= 2:
            start_rows(s - 2)
    for s in range(blocks - 2, blocks):
        start_rows(s)

    @pl.when(jnp.logical_not(outer))
    def _():
        for k in range(per + 1):
            e_copy(k).start()

    zeros = jnp.zeros((SUB, LANES), jnp.float32)
    for edge in (0, blocks + 1):

        def clear(i, _):
            for u in range(6):
                for row in range(0, rows, SUB):
                    f_ref[edge, 6 * i + u, pl.ds(TOP + row, SUB), :] = zeros
            return 0

        lax.fori_loop(0, (slices + 2 * Z0) // 6, clear, 0)
    for present, z, j0, j1 in (
        (d == 0, Z0 - 1, 0, blocks),
        (d == 1, Z0 - 1, 0, per),
        (d == 1, Z0 - 1, 2 * per - 1, 2 * per),
        (d == depths - 2, Z0 + slices, sent - 1, blocks),
        (d == depths - 1, Z0 + slices, 0, blocks),
    ):

        @pl.when(present)
        def _():
            for j in range(j0, j1):
                for row in range(0, rows, SUB):
                    f_ref[j + 1, z, pl.ds(TOP + row, SUB), :] = zeros

    for present, row in ((has_prev, TOP - SUB), (has_next, TOP + rows)):

        @pl.when(jnp.logical_not(present))
        def _():
            def clear(i, _):
                for j in range(4):
                    for z in range(slices + 2 * Z0):
                        f_ref[4 * i + j + 1, z, pl.ds(row, SUB), :] = zeros
                return 0

            lax.fori_loop(0, blocks // 4, clear, 0)

    for copy in params:
        copy.wait()
    for j in range(blocks):
        load(j).wait()
    shading = Shading(absorb, color, light)

    def relays_up(me, k, part):
        through = jnp.logical_or(k < SPLIT, jnp.logical_and(k == SPLIT, part == 0))
        inner = jnp.where(me == 1, through, jnp.logical_not(through))
        return jnp.logical_or(me == 0, jnp.logical_and(me < depths - 1, inner))

    def merges(way, k, part):
        from_below = jnp.logical_and(d > 0, relays_up(d - 1, k, part))
        from_above = jnp.logical_and(d < depths - 1, jnp.logical_not(relays_up(d + 1, k, part)))
        return jnp.logical_or(
            jnp.logical_and(way == 1, from_below), jnp.logical_and(way == 2, from_above)
        )

    def merges_any(way, k):
        return jnp.logical_or(merges(way, k, 0), merges(way, k, 1))

    def place(me, way, k):
        inner = jnp.where(way == 1, 0, jnp.where(way == 2, 2, 1))
        low = jnp.where(way == 1, 2, jnp.where(way == 2, 1, 0))
        high = jnp.where(way == 1, 1, jnp.where(way == 2, 0, 2))
        return sent + jnp.where(me == 0, low, jnp.where(me == depths - 1, high, inner)) * per + k

    parts = ((0, CUT), (CUT, rows - CUT))

    def relay_copy(up, s, k, part):
        way = jnp.where(up, 0, 1)
        at = pl.ds(*parts[part])
        return pltpu.make_async_remote_copy(
            src_ref=image.at[s, :, at, :],
            dst_ref=relay.at[way, k, :, at, :],
            send_sem=i_send.at[part, s],
            recv_sem=r_recv.at[way, k, part],
            device_id=(jnp.where(up, up_d, down_d), t),
            device_id_type=MESH,
        )

    def image_copy(way, s, k):
        up = way == 1
        owner = jnp.where(up, up_d, down_d)
        return pltpu.make_async_remote_copy(
            src_ref=image.at[s],
            dst_ref=image.at[place(owner, way, k)],
            send_sem=i_send.at[0, s],
            recv_sem=i_recv.at[way - 1, k],
            device_id=(owner, t),
            device_id_type=MESH,
        )

    def merge(way, s, k, part):
        relay_copy(way == 1, s, k, part).wait_recv()
        front = way == 1
        top, count = parts[part]
        for row in range(top, top + count, SUB):
            at = pl.ds(row, SUB)
            mine, other = image[s, 3, at, :], relay[way - 1, k, 3, at, :]
            one = jnp.ones_like(mine)
            a, b = jnp.where(front, other, one), jnp.where(front, one, mine)
            for c in range(3):
                image[s, c, at, :] = a * image[s, c, at, :] + b * relay[way - 1, k, c, at, :]
            image[s, 3, at, :] = mine * other

    def step(s, _):
        way, owner, k = order(d, s)
        j = owner * per + k
        own = way == 3
        shift = shifted(d, j)
        handed = jnp.logical_and(outer, shift)
        waited = jnp.logical_and(outer, own)

        @pl.when(jnp.logical_and(d > 0, jnp.logical_and(sends_up(d - 1, j), jnp.logical_not(waited))))
        def _():
            z_copy(0, j).wait_recv()

        @pl.when(jnp.logical_and(d < depths - 1, jnp.logical_and(sends_down(d + 1, j), jnp.logical_not(waited))))
        def _():
            z_copy(1, j).wait_recv()

        @pl.when(has_prev)
        def _():
            x_copy(0, j).wait_recv()

        @pl.when(has_next)
        def _():
            x_copy(1, j).wait_recv()

        @pl.when(jnp.logical_and(outer, s == sent))
        def _():
            for i in range(per):

                @pl.when(d == 0)
                def _():
                    z_copy(1, d * per + i).wait_recv()

                @pl.when(d > 0)
                def _():
                    z_copy(0, d * per + i).wait_recv()

            for i in range(per + 1):

                @pl.when(has_next)
                def _():
                    y_copy(0, i).start()

                @pl.when(has_prev)
                def _():
                    y_copy(1, i).start()

        keep_first = jnp.where(jnp.logical_and(d == 1, shift), 0.0, 1.0)
        keep_last = jnp.where(jnp.logical_and(d == depths - 2, shift), 0.0, 1.0)
        slot = jnp.where(own, place(d, 3, k), s)
        march(f_ref, j, image.at[slot], shading, keep_first, keep_last, slices, rows)

        @pl.when(way == 0)
        def _():
            for part in range(2):
                relay_copy(relays_up(d, k, part), s, k, part).start()

        near = jnp.logical_or(way == 1, way == 2)

        @pl.when(jnp.logical_and(near, jnp.logical_not(jnp.logical_or(handed, merges_any(way, k)))))
        def _():
            image_copy(way, s, k).start()

        late = jnp.maximum(s - LAG, 0)
        late_way, _, late_k = order(d, late)
        due = jnp.logical_and(s - LAG >= per, s - LAG < sent)

        for part in range(2):

            @pl.when(jnp.logical_and(due, merges(late_way, late_k, part)))
            def _():
                merge(late_way, late, late_k, part)

        @pl.when(jnp.logical_and(due, merges_any(late_way, late_k)))
        def _():
            image_copy(late_way, late, late_k).start()

        return 0

    lax.fori_loop(0, blocks, step, 0)

    @pl.when(outer)
    def _():
        def complete(n, _):
            i = jnp.where(d > 0, n, lax.rem(n + per, per + 1))
            j = taken(d > 0, i)
            e_wait(i)

            @pl.when(has_prev)
            def _():
                y_copy(0, i).wait_recv()

            @pl.when(has_next)
            def _():
                y_copy(1, i).wait_recv()

            away = n == 0
            s = jnp.where(d > 0, sent - 1, sent - 2)
            slot = jnp.where(away, s, place(d, 3, n - 1))
            march_one(f_ref, j, extra_z, image.at[slot], shading, d > 0, rows)

            @pl.when(away)
            def _():
                image_copy(jnp.where(d > 0, 2, 1), s, per - 1).start()

            return 0

        lax.fori_loop(0, per + 1, complete, 0)

    def drain(j, _):
        @pl.when(sends_up(d, j))
        def _():
            z_copy(0, j).wait_send()

        @pl.when(sends_down(d, j))
        def _():
            z_copy(1, j).wait_send()

        @pl.when(has_next)
        def _():
            x_copy(0, j).wait_send()

        @pl.when(has_prev)
        def _():
            x_copy(1, j).wait_send()

        return 0

    lax.fori_loop(0, blocks, drain, 0)

    for k in range(per + 1):

        @pl.when(jnp.logical_not(outer))
        def _():
            e_copy(k).wait_send()

        @pl.when(jnp.logical_and(outer, has_next))
        def _():
            y_copy(0, k).wait_send()

        @pl.when(jnp.logical_and(outer, has_prev))
        def _():
            y_copy(1, k).wait_send()

    def compose(k, _):
        for way in (1, 2):
            pltpu.make_async_remote_copy(
                src_ref=image.at[0],
                dst_ref=image.at[place(d, way, k)],
                send_sem=i_send.at[0, 0],
                recv_sem=i_recv.at[way - 1, k],
                device_id=(up_d, t),
                device_id_type=MESH,
            ).wait_recv()
        for top in range(0, rows, SUB):
            at = pl.ds(top, SUB)
            seen = image[sent + k, 3, at, :]
            total = [image[sent + k, c, at, :] for c in range(3)]
            for q in (sent + per + k, sent + 2 * per + k):
                total = [total[c] + seen * image[q, c, at, :] for c in range(3)]
                seen = seen * image[q, 3, at, :]
            for c in range(3):
                out[c, at, columns(k)] = total[c]
            out[3, at, columns(k)] = 1.0 - seen
        return 0

    lax.fori_loop(0, per, compose, 0)

    for s in range(sent):
        if s < per:
            for part in range(2):
                relay_copy(d == 0, s, 0, part).wait_send()
        else:
            image_copy(jnp.where(d >= 0, 1, 2), s, 0).wait_send()


def on_device(depths, tiles, field, absorb, color, light):
    slices, rows, columns = field.shape
    blocks = columns // LANES
    per = blocks // depths
    sent = (depths - 1) * per
    dma = pltpu.SemaphoreType.DMA
    return pl.pallas_call(
        functools.partial(kernel, depths, tiles, slices, rows, blocks),
        out_shape=pltpu.VMEM((4, rows, columns // depths), jnp.float32),
        in_specs=[pl.BlockSpec(memory_space=pl.ANY)] * 4,
        out_specs=pl.BlockSpec(memory_space=pltpu.VMEM),
        scratch_shapes=[
            pltpu.VMEM((blocks + 2, slices + 2 * Z0, rows + 2 * TOP, LANES), jnp.float32),
            pltpu.VMEM((sent + 3 * per, 4, rows, LANES), jnp.float32),
            pltpu.VMEM((2, per, 4, rows, LANES), jnp.float32),
            pltpu.SMEM((2,), jnp.float32),
            pltpu.SMEM((3, 4), jnp.float32),
            pltpu.SMEM((3,), jnp.float32),
            dma((3,)),
            dma((blocks,)),
            dma((2, blocks)),
            dma((2, blocks)),
            dma((per + 1,)),
            dma((per + 1,)),
            dma((2, blocks)),
            dma((2, blocks)),
            dma((2, per + 1)),
            dma((2, per + 1)),
            dma((2, sent)),
            dma((2, per, 2)),
            dma((2, per)),
        ],
        compiler_params=pltpu.CompilerParams(
            collective_id=0, has_side_effects=True, vmem_limit_bytes=55 << 20
        ),
    )(field, absorb, color, light)


def solution(mesh):
    depths, tiles = mesh.shape["depth"], mesh.shape["tile"]
    return jax.shard_map(
        functools.partial(on_device, depths, tiles),
        mesh=mesh,
        in_specs=(P("depth", "tile", None), P(), P(), P()),
        out_specs=P(None, "tile", "depth"),
        check_vma=False,
    )
```
